256 devices in a mesh: dp: 8 (over z_lo, x), fsdp: 16 (over y, z_hi), tensor: 2 (over core).
Axes of the slice: x: 4, y: 4, z: 8 (z_hi: 4, z_lo: 2; z = z_hi * 2 + z_lo), core: 2. Of those that a mesh axis runs over, the one named last changes fastest.
Arguments:
- fresh: bfloat16 [32768, 4608], P(('dp', 'fsdp'), 'tensor'), may hold values from -6 to 6
- replay_buffer: bfloat16 [65536, 4608], P(('dp', 'fsdp'), 'tensor'), may hold values from -6 to 6
- replay_index: int32 [32768], P(('dp', 'fsdp')), may hold values from 0 to 511
- from_replay: int32 [32768], P(('dp', 'fsdp')), may hold values 0 or 1
- cotangent: bfloat16 [32768, 2048], P(('dp', 'fsdp')), may hold values from -48 to 48
- master: float32 [2048, 4608], P(('dp', 'fsdp'), 'tensor'), may hold values from -0.09375 to 0.09375
- moment1: float32 [2048, 4608], P(('dp', 'fsdp'), 'tensor'), may hold values from -6 to 6
- moment2: float32 [2048, 4608], P(('dp', 'fsdp'), 'tensor'), may hold values from 0.25 to 4
- teacher: float32 [2048, 4608], P(('dp', 'fsdp'), 'tensor'), may hold values from -0.09375 to 0.09375
Outputs:
- new_master: float32 [2048, 4608], P(('dp', 'fsdp'), 'tensor')
- new_moment1: float32 [2048, 4608], P(('dp', 'fsdp'), 'tensor')
- new_moment2: float32 [2048, 4608], P(('dp', 'fsdp'), 'tensor')
- new_teacher: float32 [2048, 4608], P(('dp', 'fsdp'), 'tensor')
- teacher_out: float32 [32768, 2048], P(('dp', 'fsdp'), 'tensor')
The draws below stay inside these ranges and needn't reach their ends.
Inputs may be any that keep to these rules, and one draw needn't show every extreme that they name: `replay_index`: each row names a slot of its own device's block of 512 rows of replay_buffer.
All inputs are finite; a program needn't handle non-finite values. No bound on the sum of `from_replay` on one device may be relied on, other than what follows from the above.
Results may differ from the reference program's by a relative error of at most 0.004.
Values may be sent and summed in bfloat16 or wider, within the bound.
No kernel may reach another device: no remote copies, remote signals or barrier semaphores. Data moves between devices by JAX's collectives and lax.ppermute only.
A program may use at most 128 MiB of HBM per device.

```python
import math
import jax
import jax.numpy as jnp
from jax import lax

D = 4608
ROWS_DEV = 256
BUF_DEV = 512
KVW = 2048
TOKENS = 32768
SLOTS = 65536


def set_ends(drawn, stream_key, low, high):
    place = [jax.random.randint(jax.random.fold_in(stream_key, axis), (), 0, length) for axis, length in enumerate(drawn.shape)]
    widest = drawn.shape.index(max(drawn.shape))
    neighbour = place[:widest] + [(place[widest] + 1) % drawn.shape[widest]] + place[widest + 1:]
    return drawn.at[tuple(place)].set(low).at[tuple(neighbour)].set(high)


def strengthened(result, stream_key, source, target, blocks, factor):
    def block_of(position):
        return (jnp.arange(result.shape[position]) // (result.shape[position] // blocks)).reshape((-1,) + (1,) * (result.ndim - 1 - position))

    near = jax.random.permutation(stream_key, blocks)[block_of(target)]
    second = (block_of(target) + blocks // 2) % blocks
    return jnp.where((block_of(source) == near) | (block_of(source) == second), factor * result, result)


def shard_levels(stream_key, dims, shards, least, top_value):
    def one(dim, blocks):
        heights = jax.random.uniform(jax.random.fold_in(jax.random.fold_in(stream_key, 6), dim), (blocks,), jnp.float32, least / len(shards), top_value / len(shards))
        return jnp.repeat(jnp.exp(heights), dims[dim] // blocks).reshape((-1,) + (1,) * (len(dims) - dim - 1))

    loudness = one(*shards[0])
    for cut in shards[1:]:
        loudness = loudness * one(*cut)
    return loudness


def normal_values(rng, dims, scale, limit, split=(), kind=jnp.bfloat16):
    drawn = scale * jax.random.normal(rng, dims, jnp.float32)
    if split:
        drawn = drawn * shard_levels(rng, dims, split, -0.22, 0.18)
    return jnp.clip(drawn, -limit, limit).astype(kind)


def noise_with(key, dims, spread, most, shards, heavy, held_as=jnp.bfloat16):
    array = spread * jax.random.normal(key, dims, jnp.float32)
    if shards:
        array = array * shard_levels(key, dims, shards, -0.22, 0.18)
    return jnp.clip(strengthened(array, jax.random.fold_in(key, 3), *heavy), -most, most).astype(held_as)


def setup_inputs(seed: int = 0) -> dict:
    key_list = jax.random.split(jax.random.key(seed), 10)
    fresh = normal_values(key_list[0], (TOKENS, D), 1.0, 6.0, ((0, 128), (1, 2)))
    replay_buffer = normal_values(key_list[1], (SLOTS, D), 1.0, 6.0, ((0, 128), (1, 2)))
    replay_index = set_ends(jax.random.randint(key_list[2], (TOKENS,), 0, BUF_DEV), jax.random.fold_in(key_list[2], 1), 0, BUF_DEV - 1).astype(jnp.int32)
    from_replay = set_ends((jax.random.randint(key_list[3], (TOKENS,), 0, 2) < 1).astype(jnp.int32), jax.random.fold_in(key_list[3], 1), 0, 1)
    cotangent = noise_with(key_list[4], (TOKENS, KVW), 2.0, 48.0, ((0, 128),), (0, 1, 128, 5.5))
    master = normal_values(key_list[5], (KVW, D), D ** -0.5, 0.09375, ((0, 128), (1, 2)), jnp.float32)
    moment1 = normal_values(key_list[6], (KVW, D), 1.0, 6.0, ((0, 128), (1, 2)), jnp.float32)
    moment2 = jnp.clip(jnp.exp(math.log(4.0) - 2.7725887 * jax.random.uniform(key_list[7], (KVW, D), jnp.float32) ** shard_levels(key_list[7], (KVW, D), ((0, 128), (1, 2)), -0.2, 0.2)), 0.25, 4.0)
    teacher = normal_values(key_list[8], (KVW, D), D ** -0.5, 0.09375, ((0, 128), (1, 2)), jnp.float32)
    return {"fresh": fresh, "replay_buffer": replay_buffer, "replay_index": replay_index, "from_replay": from_replay, "cotangent": cotangent, "master": master, "moment1": moment1, "moment2": moment2, "teacher": teacher}


beta_one = 0.9
beta_two = 0.999
learn_rate = 0.001
adam_eps = 1e-08
ema_decay = 0.99
corr_one = 1.0 - math.exp(100.0 * math.log(0.9))
corr_two = 1.0 - math.exp(100.0 * math.log(0.999))

def reference(fresh, replay_buffer, replay_index, from_replay, cotangent, master, moment1, moment2, teacher):
    owner = jnp.arange(TOKENS, dtype=jnp.int32) // ROWS_DEV * BUF_DEV
    picked = jnp.take(replay_buffer, (owner + replay_index).astype(jnp.int32), axis=0)
    flag = (from_replay == 1)[:, None]
    student_rows = jnp.where(flag, picked, fresh)
    grad = lax.dot_general(cotangent, student_rows, (((0,), (0,)), ((), ())), preferred_element_type=jnp.float32)
    grad = grad * (1.0 / math.sqrt(TOKENS))
    new_moment1 = beta_one * moment1 + (1.0 - beta_one) * grad
    new_moment2 = beta_two * moment2 + (1.0 - beta_two) * grad * grad
    new_master = master - learn_rate * (new_moment1 / corr_one) / (jnp.sqrt(new_moment2 / corr_two) + adam_eps)
    new_teacher = ema_decay * teacher + (1.0 - ema_decay) * new_master
    gap_low = (new_master - new_teacher).astype(jnp.bfloat16)
    keys_values = lax.dot_general(picked, gap_low, (((1,), (1,)), ((), ())), preferred_element_type=jnp.float32)
    teacher_out = keys_values * from_replay.astype(jnp.float32)[:, None]
    return (new_master, new_moment1, new_moment2, new_teacher, teacher_out)
```

```python
import functools
import itertools
import math

import jax
import jax.numpy as jnp
from jax import lax
from jax.experimental import pallas as pl
from jax.experimental.pallas import tpu as pltpu
from jax.sharding import Mesh, PartitionSpec as P

beta_one = 0.9
beta_two = 0.999
learn_rate = 0.001
adam_eps = 1e-08
ema_decay = 0.99
corr_one = 1.0 - math.exp(100.0 * math.log(0.9))
corr_two = 1.0 - math.exp(100.0 * math.log(0.999))

bf16, f32 = jnp.bfloat16, jnp.float32
AXES = ("zl", "x", "y", "zh", "c")
SIZES = (2, 4, 4, 4, 2)
ROWS = tuple(AXES[:4])
VMEM_LIMIT = 48 * 1024 * 1024


def flat(zl, x, y, zh, c):
    return (((zl * 4 + x) * 4 + y) * 4 + zh) * 2 + c


def pairs(move):
    return [
        (flat(*place), flat(*move(*place)))
        for place in itertools.product(*map(range, SIZES))
    ]


def first_ring(s):
    return pairs(
        lambda zl, x, y, zh, c: (zl, (x + s) % 4, y, zh, c)
        if c == 0
        else (zl, x, (y + s) % 4, zh, c)
    )


def second_ring(s):
    return pairs(
        lambda zl, x, y, zh, c: (zl, x, (y + s) % 4, zh, c)
        if c == 0
        else (zl, (x + s) % 4, y, zh, c)
    )


other_core = pairs(lambda zl, x, y, zh, c: (zl, x, y, zh, 1 - c))


def send(array, perm):
    return lax.ppermute(array, AXES, perm)


def dot(lhs, rhs, left, right):
    return lax.dot_general(
        lhs, rhs, (((left,), (right,)), ((), ())), preferred_element_type=f32
    )


def params():
    return pltpu.CompilerParams(vmem_limit_bytes=VMEM_LIMIT)


def rows_kernel(index_ref, flag_ref, buffer_ref, fresh_ref, a_ref, b_ref):
    slots, rows = buffer_ref.shape[0], fresh_ref.shape[0]
    replayed = flag_ref[...] == 1
    slot = lax.broadcasted_iota(jnp.int32, (slots, rows), 0)
    pick = jnp.where((slot == index_ref[...]) & replayed, 1.0, 0.0).astype(bf16)
    same = lax.broadcasted_iota(jnp.int32, (rows, rows), 0) == lax.broadcasted_iota(
        jnp.int32, (rows, rows), 1
    )
    keep = jnp.where(same & jnp.logical_not(replayed), 1.0, 0.0).astype(bf16)
    got = dot(pick, buffer_ref[...], 0, 0) + dot(keep, fresh_ref[...], 0, 0)
    got = got.astype(bf16)
    a_ref[...] = got[: rows // 2]
    b_ref[...] = got[rows // 2 :]


def student_rows(index, flag, buffer, fresh):
    rows, width = fresh.shape
    block = width // 3
    half = jax.ShapeDtypeStruct((rows // 2, width), bf16)
    whole = lambda j: (0, 0)
    return pl.pallas_call(
        rows_kernel,
        grid=(3,),
        in_specs=[
            pl.BlockSpec((1, rows), whole),
            pl.BlockSpec((1, rows), whole),
            pl.BlockSpec((buffer.shape[0], block), lambda j: (0, j)),
            pl.BlockSpec((rows, block), lambda j: (0, j)),
        ],
        out_specs=[pl.BlockSpec((rows // 2, block), lambda j: (0, j))] * 2,
        out_shape=[half, half],
        compiler_params=params(),
        name="student_rows",
    )(index.reshape(1, rows), flag.reshape(1, rows), buffer, fresh)


def turn_kernel(place_ref, cot_ref, *refs):
    outs, turned = refs[:4], refs[4]
    c, p, q = place_ref[0], place_ref[1], place_ref[2]
    turned[...] = cot_ref[...].T
    for k in range(4):
        pk = (p + k) % 4
        for d in range(4):
            qd = (q + d) % 4
            x = jnp.where(c == 0, pk, qd)
            y = jnp.where(c == 0, qd, pk)
            for zl in range(2):
                start = pl.multiple_of(zl * 1024 + x * 256 + y * 64, 64)
                outs[k][pl.ds(d * 128 + zl * 64, 64), :] = turned[pl.ds(start, 64), :]


def turned_parts(place, cot):
    rows, width = cot.shape
    vmem = pl.BlockSpec(memory_space=pltpu.VMEM)
    return pl.pallas_call(
        turn_kernel,
        in_specs=[pl.BlockSpec(memory_space=pltpu.SMEM), vmem],
        out_specs=[vmem] * 4,
        out_shape=[jax.ShapeDtypeStruct((width // 4, rows), bf16)] * 4,
        scratch_shapes=[pltpu.VMEM((width, rows), bf16)],
        compiler_params=params(),
        name="turned_parts",
    )(place, cot)


def grad_kernel(*refs):
    cots, halves, outs = refs[:4], refs[4:12], refs[12:]
    total = None
    for k in range(4):
        rows = jnp.concatenate([halves[2 * k][...], halves[2 * k + 1][...]], axis=0)
        part = dot(cots[k][...], rows, 1, 0)
        total = part if total is None else total + part
    outs[0][...] = total[:128]
    for n in range(6):
        outs[n + 1][...] = total[128 + 64 * n : 192 + 64 * n].astype(bf16)


def grad_parts(cots, halves):
    rows, width = halves[0].shape
    block = width // 3
    out_shape = [jax.ShapeDtypeStruct((128, width), f32)]
    out_shape += [jax.ShapeDtypeStruct((64, width), bf16)] * 6
    return pl.pallas_call(
        grad_kernel,
        grid=(3,),
        in_specs=[pl.BlockSpec(cots[0].shape, lambda j: (0, 0))] * 4
        + [pl.BlockSpec((rows, block), lambda j: (0, j))] * 8,
        out_specs=[pl.BlockSpec((s.shape[0], block), lambda j: (0, j)) for s in out_shape],
        out_shape=out_shape,
        compiler_params=params(),
        name="grad_parts",
    )(*cots, *halves)


def values_kernel(place_ref, *refs):
    halves, gaps = refs[:8], refs[8:16]
    mine_ref, over_ref, outs = refs[16], refs[17], refs[18:21]
    gap, total = refs[21], refs[22]
    step = pl.program_id(0)
    c, q = place_ref[0], place_ref[2]
    for d in range(4):
        for zl in range(2):
            part = jnp.where(c == zl, 0, 256)
            start = pl.multiple_of(part + (q + d) % 4 * 64, 64)
            gap[pl.ds(start, 64), :] = gaps[2 * d + zl][...]
    for k in range(4):
        rows = jnp.concatenate([halves[2 * k][...], halves[2 * k + 1][...]], axis=0)
        part = dot(rows, gap[...], 1, 1)

        @pl.when(step == 0)
        def _():
            total[k] = part

        @pl.when(step > 0)
        def _():
            total[k] = total[k] + part

    @pl.when(step == pl.num_programs(0) - 1)
    def _():
        mine_ref[...] = total[0][:, :256]
        over_ref[...] = total[0][:, 256:].astype(bf16)
        for k in range(3):
            outs[k][...] = total[k + 1].astype(bf16)


def value_parts(place, halves, gaps):
    width = halves[0].shape[1]
    block = width // 3
    whole = lambda j: (0, 0)
    out_shape = [
        jax.ShapeDtypeStruct((256, 256), f32),
        jax.ShapeDtypeStruct((256, 256), bf16),
    ] + [jax.ShapeDtypeStruct((256, 512), bf16)] * 3
    return pl.pallas_call(
        values_kernel,
        grid=(3,),
        in_specs=[pl.BlockSpec(memory_space=pltpu.SMEM)]
        + [pl.BlockSpec((128, block), lambda j: (0, j))] * 8
        + [pl.BlockSpec((64, block), lambda j: (0, j))] * 8,
        out_specs=[pl.BlockSpec(s.shape, whole) for s in out_shape],
        out_shape=out_shape,
        scratch_shapes=[pltpu.VMEM((512, block), bf16), pltpu.VMEM((4, 256, 512), f32)],
        compiler_params=params(),
        name="value_parts",
    )(place, *halves, *gaps)


def join_kernel(place_ref, flag_ref, *refs):
    mine, over, out_ref, held = refs[:4], refs[4], refs[5], refs[6]
    c, p, q = place_ref[0], place_ref[1], place_ref[2]
    for d in range(4):
        held[c, (p + d) % 4] = mine[d][:, :256].astype(f32)
        held[1 - c, (q + d) % 4] = over[d].astype(f32)
    flag = flag_ref[...].astype(f32)
    for x in range(4):
        for j in range(2):
            near = held[0, x, :, j * 128 : (j + 1) * 128]
            far = jnp.concatenate(
                [
                    held[1, 2 * j, :, x * 64 : (x + 1) * 64],
                    held[1, 2 * j + 1, :, x * 64 : (x + 1) * 64],
                ],
                axis=1,
            )
            out_ref[:, x * 256 + j * 128 : x * 256 + (j + 1) * 128] = (near + far) * flag


def joined(place, flag, mine, over):
    vmem = pl.BlockSpec(memory_space=pltpu.VMEM)
    return pl.pallas_call(
        join_kernel,
        in_specs=[pl.BlockSpec(memory_space=pltpu.SMEM)] + [vmem] * 6,
        out_specs=vmem,
        out_shape=jax.ShapeDtypeStruct((256, 1024), f32),
        scratch_shapes=[pltpu.VMEM((2, 4, 256, 256), f32)],
        compiler_params=params(),
        name="joined",
    )(place, flag.reshape(256, 1), *mine, over)


def body(
    fresh, replay_buffer, replay_index, from_replay, cotangent, master, moment1, moment2, teacher
):
    c, x, y = (lax.axis_index(a) for a in ("c", "x", "y"))
    p = jnp.where(c == 0, x, y)
    q = jnp.where(c == 0, y, x)
    place = jnp.stack([c, p, q]).astype(jnp.int32)
    total_rows = fresh.shape[0] * lax.axis_size(ROWS)

    a, b = student_rows(replay_index, from_replay, replay_buffer, fresh)
    up, down = first_ring(1), first_ring(-1)
    left_a = send(a, up)
    right_b = send(b, down)
    left_b = send(b, up)
    right_a = send(a, down)
    cots = turned_parts(place, cotangent)
    far_a = send(left_a, up)
    far_b = send(right_b, down)
    cot_left = send(cots[1], up)
    cot_far = send(cots[2], first_ring(2))
    cot_right = send(cots[3], down)
    halves = (a, b, right_a, right_b, left_a, left_b, far_a, far_b)
    own, a1, b1, a2, b2, am, bm = grad_parts((cots[0], cot_right, cot_left, cot_far), halves)

    up2, down2 = second_ring(1), second_ring(-1)
    pass_a = send(a2, up2)
    pass_b = send(b2, down2)
    got_b = send(b1, up2)
    got_a = send(am, down2)
    sum_a = send((a1.astype(f32) + pass_a.astype(f32)).astype(bf16), up2)
    sum_b = send((bm.astype(f32) + pass_b.astype(f32)).astype(bf16), down2)
    ring_sum = jnp.concatenate(
        [
            own[:64] + sum_a.astype(f32) + got_a.astype(f32),
            own[64:] + sum_b.astype(f32) + got_b.astype(f32),
        ],
        axis=0,
    ).astype(bf16)

    width = own.shape[1]
    slices = lax.all_to_all(ring_sum.reshape(8, 16, width), ("zl", "zh"), 0, 0, tiled=True)
    grad = jnp.sum(slices.astype(f32), axis=0)
    grad = grad * (1.0 / math.sqrt(total_rows))
    new_moment1 = beta_one * moment1 + (1.0 - beta_one) * grad
    new_moment2 = beta_two * moment2 + (1.0 - beta_two) * grad * grad
    new_master = master - learn_rate * (new_moment1 / corr_one) / (
        jnp.sqrt(new_moment2 / corr_two) + adam_eps
    )
    new_teacher = ema_decay * teacher + (1.0 - ema_decay) * new_master
    gap_low = (new_master - new_teacher).astype(bf16)

    copies = jnp.broadcast_to(gap_low[None], (8, 16, width))
    column = lax.all_to_all(copies, ("zl", "zh"), 0, 0, tiled=True)
    ga = column[:4].reshape(64, width)
    gb = column[4:].reshape(64, width)
    left_ga = send(ga, up2)
    right_gb = send(gb, down2)
    left_gb = send(gb, up2)
    right_ga = send(ga, down2)
    far_ga = send(left_ga, up2)
    far_gb = send(right_gb, down2)
    gaps = (ga, gb, right_ga, right_gb, far_ga, far_gb, left_ga, left_gb)
    mine, over, out_right, out_left, out_far = value_parts(place, halves, gaps)

    from_far = send(out_far, first_ring(2))
    from_left = send(out_right, up)
    from_right = send(out_left, down)
    crossing = jnp.stack([over, from_right[:, 256:], from_far[:, 256:], from_left[:, 256:]])
    crossed = send(crossing, other_core)
    teacher_out = joined(
        place, from_replay, (mine, from_right, from_far, from_left), crossed
    )
    return (new_master, new_moment1, new_moment2, new_teacher, teacher_out)


def solution(mesh):
    fine = Mesh(mesh.devices.reshape(SIZES), AXES)
    split = P(ROWS, "c")
    return jax.shard_map(
        body,
        mesh=fine,
        in_specs=(split, split, P(ROWS), P(ROWS), P(ROWS, None), split, split, split, split),
        out_specs=(split, split, split, split, split),
        check_vma=False,
    )
```

```python
import functools
import itertools
import math

import jax
import jax.numpy as jnp
from jax import lax
from jax.experimental import pallas as pl
from jax.experimental.pallas import tpu as pltpu
from jax.sharding import Mesh, PartitionSpec as P

beta_one = 0.9
beta_two = 0.999
learn_rate = 0.001
adam_eps = 1e-08
ema_decay = 0.99
corr_one = 1.0 - math.exp(100.0 * math.log(0.9))
corr_two = 1.0 - math.exp(100.0 * math.log(0.999))

bf16, f32 = jnp.bfloat16, jnp.float32
AXES = ("zl", "x", "y", "zh", "c")
SIZES = (2, 4, 4, 4, 2)
ROWS = tuple(AXES[:4])
VMEM_LIMIT = 16 * 1024 * 1024
SHARE_LIMIT = 52 * 1024 * 1024


def flat(zl, x, y, zh, c):
    return (((zl * 4 + x) * 4 + y) * 4 + zh) * 2 + c


def pairs(move):
    return [
        (flat(*place), flat(*move(*place)))
        for place in itertools.product(*map(range, SIZES))
    ]


def first_ring(s):
    return pairs(
        lambda zl, x, y, zh, c: (zl, (x + s) % 4, y, zh, c)
        if c == 0
        else (zl, x, (y + s) % 4, zh, c)
    )


def second_ring(s):
    return pairs(
        lambda zl, x, y, zh, c: (zl, x, (y + s) % 4, zh, c)
        if c == 0
        else (zl, (x + s) % 4, y, zh, c)
    )


other_core = pairs(lambda zl, x, y, zh, c: (zl, x, y, zh, 1 - c))


def send(array, perm):
    return lax.ppermute(array, AXES, perm)


def dot(lhs, rhs, left, right):
    return lax.dot_general(
        lhs, rhs, (((left,), (right,)), ((), ())), preferred_element_type=f32
    )


def params():
    return pltpu.CompilerParams(vmem_limit_bytes=VMEM_LIMIT)


def cost(flops, size):
    return pl.CostEstimate(flops=flops, bytes_accessed=size, transcendentals=0)


def in_vmem(count):
    return [pl.BlockSpec(memory_space=pltpu.VMEM)] * count


def scalars():
    return [pl.BlockSpec(memory_space=pltpu.SMEM)]


COLS = 256


def share_kernel(*refs):
    place_ref, slot_ref, buffer_hbm, fresh_hbm, cot_hbm = refs[:5]
    a_ref, b_ref, up_ref, down_ref, own_ref, far_ref = refs[5:11]
    buffer_ref, fresh_ref, cot_ref, turned, sems = refs[11:]
    slots, rows = buffer_ref.shape[0], fresh_ref.shape[0]
    width, half = fresh_ref.shape[1], fresh_ref.shape[0] // 2
    third = width // 3
    cot_copy = pltpu.make_async_copy(cot_hbm, cot_ref, sems.at[0])
    large = []
    for j in range(3):
        cut = (slice(None), pl.ds(j * third, third))
        large.append(
            (
                pltpu.make_async_copy(fresh_hbm.at[cut], fresh_ref.at[cut], sems.at[1 + j]),
                pltpu.make_async_copy(buffer_hbm.at[cut], buffer_ref.at[cut], sems.at[4 + j]),
            )
        )
    for copy in [cot_copy] + [copy for pair in large for copy in pair]:
        copy.start()

    wanted = slot_ref[...]
    slot = lax.broadcasted_iota(jnp.int32, (slots, rows), 0)
    pick = jnp.where(slot == wanted, 1.0, 0.0).astype(bf16).T
    same = lax.broadcasted_iota(jnp.int32, (rows, rows), 0) == lax.broadcasted_iota(
        jnp.int32, (rows, rows), 1
    )
    keep = jnp.where(same & (wanted < 0), 1.0, 0.0).astype(bf16).T

    cot_copy.wait()
    turned[...] = cot_ref[...].T
    c, p, q = place_ref[0], place_ref[1], place_ref[2]
    blocks = width // COLS
    cots = (
        own_ref,
        up_ref.at[pl.ds(blocks * half, 512)],
        far_ref,
        down_ref.at[pl.ds(blocks * half, 512)],
    )
    for k in range(4):
        pk = (p + k) % 4
        for d in range(4):
            qd = (q + d) % 4
            x = jnp.where(c == 0, pk, qd)
            y = jnp.where(c == 0, qd, pk)
            for zl in range(2):
                start = pl.multiple_of(zl * 1024 + x * 256 + y * 64, 64)
                cots[k][pl.ds(d * 128 + zl * 64, 64), :] = turned[pl.ds(start, 64), :]

    for j in range(blocks):
        if j % (blocks // 3) == 0:
            for copy in large[j // (blocks // 3)]:
                copy.wait()
        cut = (slice(None), pl.ds(j * COLS, COLS))
        got = dot(pick, buffer_ref[cut], 1, 0) + dot(keep, fresh_ref[cut], 1, 0)
        got = got.astype(bf16)
        at = pl.ds(j * half, half)
        a_ref[at, :] = got[:half]
        down_ref[at, :] = got[:half]
        b_ref[at, :] = got[half:]
        up_ref[at, :] = got[half:]


def shared(place, slot, buffer, fresh, cot):
    rows, width = fresh.shape
    tall = width // COLS * (rows // 2)
    shapes = [(tall, COLS)] * 2 + [(tall + 512, COLS)] * 2 + [(512, rows)] * 2
    hbm = pl.BlockSpec(memory_space=pl.ANY)
    return pl.pallas_call(
        share_kernel,
        in_specs=scalars() + in_vmem(1) + [hbm] * 3,
        out_specs=in_vmem(6),
        out_shape=[jax.ShapeDtypeStruct(shape, bf16) for shape in shapes],
        scratch_shapes=[
            pltpu.VMEM(buffer.shape, bf16),
            pltpu.VMEM(fresh.shape, bf16),
            pltpu.VMEM(cot.shape, bf16),
            pltpu.VMEM((cot.shape[1], rows), bf16),
            pltpu.SemaphoreType.DMA((7,)),
        ],
        compiler_params=pltpu.CompilerParams(vmem_limit_bytes=SHARE_LIMIT),
        cost_estimate=cost(2 * 768 * rows * width, 8 * rows * width),
        name="shared",
    )(place, slot, buffer, fresh, cot)


def column_block(half, j):
    return half[pl.ds(pl.multiple_of(j * 128, 128), 128), :]


def all_columns(half):
    return jnp.concatenate([half[128 * j : 128 * (j + 1), :] for j in range(9)], axis=1)


def near_kernel(own_ref, *refs):
    halves, out_ref = refs[:6], refs[6]
    carried = halves[0].shape[0]
    cots = (own_ref, halves[2].at[pl.ds(carried, 512)], halves[5].at[pl.ds(carried, 512)])

    @pl.loop(0, out_ref.shape[1] // COLS)
    def _(j):
        total = None
        for k in range(3):
            rows = jnp.concatenate(
                [column_block(halves[2 * k], j), column_block(halves[2 * k + 1], j)], axis=0
            )
            part = dot(cots[k][...], rows, 1, 0)
            total = part if total is None else total + part
        out_ref[:, pl.ds(pl.multiple_of(j * COLS, COLS), COLS)] = total


def near_grad(cot, halves):
    width = halves[0].shape[0] // 128 * COLS
    return pl.pallas_call(
        near_kernel,
        in_specs=in_vmem(7),
        out_specs=in_vmem(1)[0],
        out_shape=jax.ShapeDtypeStruct((512, width), f32),
        compiler_params=params(),
        cost_estimate=cost(2 * 768 * 512 * width, 8 * 512 * width),
        name="near_grad",
    )(cot, *halves)


def far_kernel(starts, near_ref, cot_ref, a_ref, b_ref, *outs):
    @pl.loop(0, near_ref.shape[1] // COLS)
    def _(j):
        cut = (slice(None), pl.ds(pl.multiple_of(j * COLS, COLS), COLS))
        rows = jnp.concatenate([column_block(a_ref, j), column_block(b_ref, j)], axis=0)
        sums = {}
        for start, out in zip(starts, outs):
            chunk, low = start // 128, start % 128
            if chunk not in sums:
                at = slice(128 * chunk, 128 * chunk + 128)
                sums[chunk] = near_ref[at, cut[1]] + dot(cot_ref[at, :], rows, 1, 0)
            out[cut] = sums[chunk][low : low + out.shape[0]].astype(out.dtype)


def grad_parts(starts, near, cot, a, b):
    width = near.shape[1]
    out_shape = [
        jax.ShapeDtypeStruct((64, width), bf16)
        if start
        else jax.ShapeDtypeStruct((128, width), f32)
        for start in starts
    ]
    return pl.pallas_call(
        functools.partial(far_kernel, starts),
        in_specs=in_vmem(4),
        out_specs=in_vmem(len(starts)),
        out_shape=out_shape,
        compiler_params=params(),
        cost_estimate=cost(2 * 256 * 64 * len(starts) * width, 4 * 512 * width),
        name="grad_parts",
    )(near, cot, a, b)


def own_first(c, a, b):
    return [jnp.where(c == 0, a, b), jnp.where(c == 0, b, a)]


def values_kernel(groups, place_ref, *refs):
    halves, gaps, out_ref = refs[:8], refs[8 : 8 + 2 * groups], refs[8 + 2 * groups]
    c = place_ref[0]
    gap = []
    for n in range(groups):
        gap += own_first(c, gaps[2 * n][...], gaps[2 * n + 1][...])
    gap = jnp.concatenate(gap, axis=0)
    for k in range(4):
        rows = jnp.concatenate(
            [all_columns(halves[2 * k]), all_columns(halves[2 * k + 1])], axis=0
        )
        out_ref[pl.ds(256 * k, 256), :] = dot(rows, gap, 1, 1)


def values(place, halves, gaps):
    groups, width = len(gaps) // 2, gaps[0].shape[1]
    return pl.pallas_call(
        functools.partial(values_kernel, groups),
        in_specs=scalars() + in_vmem(len(halves) + len(gaps)),
        out_specs=in_vmem(1)[0],
        out_shape=jax.ShapeDtypeStruct((1024, 128 * groups), f32),
        compiler_params=params(),
        cost_estimate=cost(2 * 1024 * 128 * groups * width, 4 * 1024 * width),
        name="values",
    )(place, *halves, *gaps)


def packed(q, tiles):
    pairs_of = lambda left, right, lo: jnp.concatenate(
        [left[:, lo : lo + 64], right[:, lo : lo + 64]], axis=1
    )
    both = []
    for lo in (0, 64):
        line = jnp.concatenate(
            [pairs_of(tiles[0], tiles[1], lo), pairs_of(tiles[2], tiles[3], lo)], axis=1
        )
        both.append(pltpu.roll(line, q * 64, 1))
    return both


def last_kernel(devices, place_ref, own_ref, side_ref, *refs):
    count = len(devices)
    halves, gaps, outs = refs[: 2 * count], refs[2 * count : 2 * count + 2], refs[2 * count + 2 :]
    c, q = place_ref[0], place_ref[2]
    gap = jnp.concatenate(own_first(c, gaps[0][...], gaps[1][...]), axis=0)
    for n, k in enumerate(devices):
        rows = jnp.concatenate(
            [all_columns(halves[2 * n]), all_columns(halves[2 * n + 1])], axis=0
        )
        part = dot(rows, gap, 1, 1)
        cut = pl.ds(256 * k, 256)
        side = side_ref[cut, :]
        mine, over = packed(q, (own_ref[cut, :], side[:, :128], part, side[:, 128:]))
        if k == 0:
            outs[n][...] = mine
            outs[n + 1][...] = over.astype(bf16)
        else:
            outs[n][:, :256] = mine.astype(bf16)
            outs[n][:, 256:] = over.astype(bf16)


def value_parts(devices, place, own, side, halves, gaps):
    width = gaps[0].shape[1]
    out_shape = []
    for k in devices:
        if k == 0:
            out_shape.append(jax.ShapeDtypeStruct((256, 256), f32))
            out_shape.append(jax.ShapeDtypeStruct((256, 256), bf16))
        else:
            out_shape.append(jax.ShapeDtypeStruct((256, 512), bf16))
    taken = [half for k in devices for half in halves[2 * k : 2 * k + 2]]
    return pl.pallas_call(
        functools.partial(last_kernel, devices),
        in_specs=scalars() + in_vmem(4 + len(taken)),
        out_specs=in_vmem(len(out_shape)),
        out_shape=out_shape,
        compiler_params=params(),
        cost_estimate=cost(2 * 256 * len(devices) * 128 * width, 1024 * width),
        name="value_parts",
    )(place, own, side, *taken, *gaps)


def join_kernel(place_ref, flag_ref, *refs):
    mine, over, out_ref, held = refs[:4], refs[4:8], refs[8], refs[9]
    c, p, q = place_ref[0], place_ref[1], place_ref[2]
    for d in range(4):
        held[c, (p + d) % 4] = mine[d][:, :256].astype(f32)
        held[1 - c, (q + d) % 4] = over[d][:, -256:].astype(f32)
    flag = flag_ref[...].astype(f32)
    for x in range(4):
        for j in range(2):
            near = held[0, x, :, j * 128 : (j + 1) * 128]
            far = jnp.concatenate(
                [
                    held[1, 2 * j, :, x * 64 : (x + 1) * 64],
                    held[1, 2 * j + 1, :, x * 64 : (x + 1) * 64],
                ],
                axis=1,
            )
            out_ref[:, x * 256 + j * 128 : x * 256 + (j + 1) * 128] = (near + far) * flag


def joined(place, flag, mine, over):
    vmem = pl.BlockSpec(memory_space=pltpu.VMEM)
    return pl.pallas_call(
        join_kernel,
        in_specs=[pl.BlockSpec(memory_space=pltpu.SMEM)] + [vmem] * 9,
        out_specs=vmem,
        out_shape=jax.ShapeDtypeStruct((256, 1024), f32),
        scratch_shapes=[pltpu.VMEM((2, 4, 256, 256), f32)],
        compiler_params=params(),
        name="joined",
    )(place, flag.reshape(256, 1), *mine, *over)


def body(
    fresh, replay_buffer, replay_index, from_replay, cotangent, master, moment1, moment2, teacher
):
    c, x, y = (lax.axis_index(a) for a in ("c", "x", "y"))
    p = jnp.where(c == 0, x, y)
    q = jnp.where(c == 0, y, x)
    place = jnp.stack([c, p, q]).astype(jnp.int32)
    total_rows = fresh.shape[0] * lax.axis_size(ROWS)

    up, down = first_ring(1), first_ring(-1)
    slot = jnp.where(from_replay == 1, replay_index, -1).reshape(1, -1)
    a, b, b_cot, a_cot, cot_own, cot_over = shared(
        place, slot, replay_buffer, fresh, cotangent
    )
    left_a = send(a, up)
    right_b = send(b, down)
    left_b = send(b_cot, up)
    right_a = send(a_cot, down)
    cot_far = send(cot_over, first_ring(2))
    far_a = send(left_a, up)
    far_b = send(right_b, down)
    halves = (a, b, right_a, right_b, left_a, left_b, far_a, far_b)
    near = near_grad(cot_own, halves[:6])
    far = (near, cot_far, far_a, far_b)
    a2, b2 = grad_parts((256, 320), *far)
    am, bm, b1, a1, own = grad_parts((384, 448, 192, 128, 0), *far)

    up2, down2 = second_ring(1), second_ring(-1)
    pass_a = send(a2, up2)
    pass_b = send(b2, down2)
    got_b = send(b1, up2)
    got_a = send(am, down2)
    sum_a = send((a1.astype(f32) + pass_a.astype(f32)).astype(bf16), up2)
    sum_b = send((bm.astype(f32) + pass_b.astype(f32)).astype(bf16), down2)
    ring_sum = jnp.concatenate(
        [
            own[:64] + sum_a.astype(f32) + got_a.astype(f32),
            own[64:] + sum_b.astype(f32) + got_b.astype(f32),
        ],
        axis=0,
    ).astype(bf16)

    width = own.shape[1]
    slices = lax.all_to_all(ring_sum.reshape(8, 16, width), ("zl", "zh"), 0, 0, tiled=True)
    grad = jnp.sum(slices.astype(f32), axis=0)
    grad = grad * (1.0 / math.sqrt(total_rows))
    new_moment1 = beta_one * moment1 + (1.0 - beta_one) * grad
    new_moment2 = beta_two * moment2 + (1.0 - beta_two) * grad * grad
    new_master = master - learn_rate * (new_moment1 / corr_one) / (
        jnp.sqrt(new_moment2 / corr_two) + adam_eps
    )
    new_teacher = ema_decay * teacher + (1.0 - ema_decay) * new_master
    gap_low = (new_master - new_teacher).astype(bf16)

    copies = jnp.broadcast_to(gap_low[None], (8, 16, width))
    column = lax.all_to_all(copies, ("zl", "zh"), 0, 0, tiled=True)
    ga = column[:4].reshape(64, width)
    gb = column[4:].reshape(64, width)
    left_ga = send(ga, up2)
    right_gb = send(gb, down2)
    left_gb = send(gb, up2)
    right_ga = send(ga, down2)
    far_ga = send(left_ga, up2)
    far_gb = send(right_gb, down2)
    first = values(place, halves, (ga, gb))
    side = values(place, halves, (right_ga, right_gb, left_ga, left_gb))
    known = (place, first, side, halves, (far_ga, far_gb))

    (out_far,) = value_parts((3,), *known)
    from_far = send(out_far, first_ring(2))
    out_right, out_left, mine, over = value_parts((1, 2, 0), *known)
    from_left = send(out_right, up)
    from_right = send(out_left, down)
    got = (from_right, from_far, from_left)
    crossed = [send(part, other_core) for part in (over,) + got]
    teacher_out = joined(place, from_replay, (mine,) + got, crossed)
    return (new_master, new_moment1, new_moment2, new_teacher, teacher_out)


def solution(mesh):
    fine = Mesh(mesh.devices.reshape(SIZES), AXES)
    split = P(ROWS, "c")
    return jax.shard_map(
        body,
        mesh=fine,
        in_specs=(split, split, P(ROWS), P(ROWS), P(ROWS, None), split, split, split, split),
        out_specs=(split, split, split, split, split),
        check_vma=False,
    )
```

```python
import functools
import itertools
import math

import jax
import jax.numpy as jnp
from jax import lax
from jax.experimental import pallas as pl
from jax.experimental.pallas import tpu as pltpu
from jax.sharding import Mesh, PartitionSpec as P

beta_one = 0.9
beta_two = 0.999
learn_rate = 0.001
adam_eps = 1e-08
ema_decay = 0.99
corr_one = 1.0 - math.exp(100.0 * math.log(0.9))
corr_two = 1.0 - math.exp(100.0 * math.log(0.999))

bf16, f32 = jnp.bfloat16, jnp.float32
AXES = ("zl", "x", "y", "zh", "c")
SIZES = (2, 4, 4, 4, 2)
ROWS = tuple(AXES[:4])
VMEM_LIMIT = 16 * 1024 * 1024
SHARE_LIMIT = 50 * 1024 * 1024


def flat(zl, x, y, zh, c):
    return (((zl * 4 + x) * 4 + y) * 4 + zh) * 2 + c


def pairs(move):
    return [
        (flat(*place), flat(*move(*place)))
        for place in itertools.product(*map(range, SIZES))
    ]


def first_ring(s):
    return pairs(
        lambda zl, x, y, zh, c: (zl, (x + s) % 4, y, zh, c)
        if c == 0
        else (zl, x, (y + s) % 4, zh, c)
    )


def second_ring(s):
    return pairs(
        lambda zl, x, y, zh, c: (zl, x, (y + s) % 4, zh, c)
        if c == 0
        else (zl, (x + s) % 4, y, zh, c)
    )


other_core = pairs(lambda zl, x, y, zh, c: (zl, x, y, zh, 1 - c))


def send(array, perm):
    return lax.ppermute(array, AXES, perm)


def dot(lhs, rhs, left, right):
    return lax.dot_general(
        lhs, rhs, (((left,), (right,)), ((), ())), preferred_element_type=f32
    )


def params():
    return pltpu.CompilerParams(vmem_limit_bytes=VMEM_LIMIT)


def cost(flops, size):
    return pl.CostEstimate(flops=flops, bytes_accessed=size, transcendentals=0)


def in_vmem(count):
    return [pl.BlockSpec(memory_space=pltpu.VMEM)] * count


def scalars():
    return [pl.BlockSpec(memory_space=pltpu.SMEM)]


COLS = 256
WIDTH = 2304
TALL = WIDTH // COLS * 128


def share_kernel(*refs):
    place_ref, slot_ref, buffer_hbm, fresh_hbm, cot_hbm = refs[:5]
    a_ref, b_ref, up_ref, down_ref, own_ref = refs[5:10]
    buffer_ref, fresh_ref, cot_ref, turned, sems = refs[10:]
    slots, rows = buffer_ref.shape[0], fresh_ref.shape[0]
    width, half = fresh_ref.shape[1], fresh_ref.shape[0] // 2
    third = width // 3
    cot_copy = pltpu.make_async_copy(cot_hbm, cot_ref, sems.at[0])
    large = []
    for j in range(3):
        cut = (slice(None), pl.ds(j * third, third))
        large.append(
            (
                pltpu.make_async_copy(fresh_hbm.at[cut], fresh_ref.at[cut], sems.at[1 + j]),
                pltpu.make_async_copy(buffer_hbm.at[cut], buffer_ref.at[cut], sems.at[4 + j]),
            )
        )
    for copy in [cot_copy] + [copy for pair in large for copy in pair]:
        copy.start()

    wanted = slot_ref[...]
    slot = lax.broadcasted_iota(jnp.int32, (slots, rows), 0)
    pick = jnp.where(slot == wanted, 1.0, 0.0).astype(bf16).T
    same = lax.broadcasted_iota(jnp.int32, (rows, rows), 0) == lax.broadcasted_iota(
        jnp.int32, (rows, rows), 1
    )
    keep = jnp.where(same & (wanted < 0), 1.0, 0.0).astype(bf16).T

    cot_copy.wait()
    turned[...] = cot_ref[...].T
    c, p, q = place_ref[0], place_ref[1], place_ref[2]
    blocks = width // COLS
    for k in range(4):
        pk = (p + k) % 4
        for d in range(4):
            qd = (q + d) % 4
            x = jnp.where(c == 0, pk, qd)
            y = jnp.where(c == 0, qd, pk)
            if k == 2:
                target, base = (a_ref, b_ref)[d // 2], TALL + d % 2 * 128
            elif k == 0:
                target, base = own_ref, d * 128
            else:
                target, base = up_ref if k == 1 else down_ref, TALL + d * 128
            for zl in range(2):
                start = pl.multiple_of(zl * 1024 + x * 256 + y * 64, 64)
                target[pl.ds(base + zl * 64, 64), :] = turned[pl.ds(start, 64), :]

    for j in range(blocks):
        if j % (blocks // 3) == 0:
            for copy in large[j // (blocks // 3)]:
                copy.wait()
        cut = (slice(None), pl.ds(j * COLS, COLS))
        got = dot(pick, buffer_ref[cut], 1, 0) + dot(keep, fresh_ref[cut], 1, 0)
        got = got.astype(bf16)
        at = pl.ds(j * half, half)
        a_ref[at, :] = got[:half]
        down_ref[at, :] = got[:half]
        b_ref[at, :] = got[half:]
        up_ref[at, :] = got[half:]


def shared(place, slot, buffer, fresh, cot):
    rows, width = fresh.shape
    shapes = [(TALL + 256, COLS)] * 2 + [(TALL + 512, COLS)] * 2 + [(512, rows)]
    hbm = pl.BlockSpec(memory_space=pl.ANY)
    return pl.pallas_call(
        share_kernel,
        in_specs=scalars() + in_vmem(1) + [hbm] * 3,
        out_specs=in_vmem(5),
        out_shape=[jax.ShapeDtypeStruct(shape, bf16) for shape in shapes],
        scratch_shapes=[
            pltpu.VMEM(buffer.shape, bf16),
            pltpu.VMEM(fresh.shape, bf16),
            pltpu.VMEM(cot.shape, bf16),
            pltpu.VMEM((cot.shape[1], rows), bf16),
            pltpu.SemaphoreType.DMA((7,)),
        ],
        compiler_params=pltpu.CompilerParams(vmem_limit_bytes=SHARE_LIMIT),
        cost_estimate=cost(2 * 768 * rows * width, 8 * rows * width),
        name="shared",
    )(place, slot, buffer, fresh, cot)


def column_block(half, j):
    return half[pl.ds(pl.multiple_of(j * 128, 128), 128), :]


def all_columns(half):
    return jnp.concatenate([half[128 * j : 128 * (j + 1), :] for j in range(9)], axis=1)


def near_kernel(own_ref, *refs):
    halves, out_ref = refs[:6], refs[6]
    cots = (own_ref, halves[2].at[pl.ds(TALL, 512)], halves[5].at[pl.ds(TALL, 512)])

    @pl.loop(0, out_ref.shape[1] // COLS)
    def _(j):
        total = None
        for k in range(3):
            rows = jnp.concatenate(
                [column_block(halves[2 * k], j), column_block(halves[2 * k + 1], j)], axis=0
            )
            part = dot(cots[k][...], rows, 1, 0)
            total = part if total is None else total + part
        out_ref[:, pl.ds(pl.multiple_of(j * COLS, COLS), COLS)] = total


def near_grad(cot, halves):
    width = WIDTH
    return pl.pallas_call(
        near_kernel,
        in_specs=in_vmem(7),
        out_specs=in_vmem(1)[0],
        out_shape=jax.ShapeDtypeStruct((512, width), f32),
        compiler_params=params(),
        cost_estimate=cost(2 * 768 * 512 * width, 8 * 512 * width),
        name="near_grad",
    )(cot, *halves)


def far_kernel(starts, near_ref, a_ref, b_ref, *outs):
    @pl.loop(0, near_ref.shape[1] // COLS)
    def _(j):
        cut = (slice(None), pl.ds(pl.multiple_of(j * COLS, COLS), COLS))
        rows = jnp.concatenate([column_block(a_ref, j), column_block(b_ref, j)], axis=0)
        sums = {}
        for start, out in zip(starts, outs):
            chunk, low = start // 128, start % 128
            if chunk not in sums:
                at = slice(128 * chunk, 128 * chunk + 128)
                cot = (a_ref, b_ref)[chunk // 2][pl.ds(TALL + chunk % 2 * 128, 128), :]
                sums[chunk] = near_ref[at, cut[1]] + dot(cot, rows, 1, 0)
            out[cut] = sums[chunk][low : low + out.shape[0]].astype(out.dtype)


def grad_parts(starts, near, a, b):
    width = near.shape[1]
    out_shape = [
        jax.ShapeDtypeStruct((64, width), bf16)
        if start
        else jax.ShapeDtypeStruct((128, width), f32)
        for start in starts
    ]
    return pl.pallas_call(
        functools.partial(far_kernel, starts),
        in_specs=in_vmem(3),
        out_specs=in_vmem(len(starts)),
        out_shape=out_shape,
        compiler_params=params(),
        cost_estimate=cost(2 * 256 * 64 * len(starts) * width, 4 * 512 * width),
        name="grad_parts",
    )(near, a, b)


def own_first(c, a, b):
    return [jnp.where(c == 0, a, b), jnp.where(c == 0, b, a)]


def values_kernel(groups, place_ref, *refs):
    halves, gaps, out_ref = refs[:8], refs[8 : 8 + 2 * groups], refs[8 + 2 * groups]
    c = place_ref[0]
    gap = []
    for n in range(groups):
        gap += own_first(c, gaps[2 * n][...], gaps[2 * n + 1][...])
    gap = jnp.concatenate(gap, axis=0)
    for k in range(4):
        rows = jnp.concatenate(
            [all_columns(halves[2 * k]), all_columns(halves[2 * k + 1])], axis=0
        )
        out_ref[pl.ds(256 * k, 256), :] = dot(rows, gap, 1, 1)


def values(place, halves, gaps):
    groups, width = len(gaps) // 2, gaps[0].shape[1]
    return pl.pallas_call(
        functools.partial(values_kernel, groups),
        in_specs=scalars() + in_vmem(len(halves) + len(gaps)),
        out_specs=in_vmem(1)[0],
        out_shape=jax.ShapeDtypeStruct((1024, 128 * groups), f32),
        compiler_params=params(),
        cost_estimate=cost(2 * 1024 * 128 * groups * width, 4 * 1024 * width),
        name="values",
    )(place, *halves, *gaps)


def packed(q, tiles):
    pairs_of = lambda left, right, lo: jnp.concatenate(
        [left[:, lo : lo + 64], right[:, lo : lo + 64]], axis=1
    )
    both = []
    for lo in (0, 64):
        line = jnp.concatenate(
            [pairs_of(tiles[0], tiles[1], lo), pairs_of(tiles[2], tiles[3], lo)], axis=1
        )
        both.append(pltpu.roll(line, q * 64, 1))
    return both


def last_kernel(devices, place_ref, own_ref, side_ref, *refs):
    count = len(devices)
    halves, gaps, outs = refs[: 2 * count], refs[2 * count : 2 * count + 2], refs[2 * count + 2 :]
    c, q = place_ref[0], place_ref[2]
    gap = jnp.concatenate(own_first(c, gaps[0][...], gaps[1][...]), axis=0)
    for n, k in enumerate(devices):
        rows = jnp.concatenate(
            [all_columns(halves[2 * n]), all_columns(halves[2 * n + 1])], axis=0
        )
        part = dot(rows, gap, 1, 1)
        cut = pl.ds(256 * k, 256)
        side = side_ref[cut, :]
        mine, over = packed(q, (own_ref[cut, :], side[:, :128], part, side[:, 128:]))
        if k == 0:
            outs[n][...] = mine
            outs[n + 1][...] = over.astype(bf16)
        else:
            outs[n][:, :256] = mine.astype(bf16)
            outs[n][:, 256:] = over.astype(bf16)


def value_parts(devices, place, own, side, halves, gaps):
    width = gaps[0].shape[1]
    out_shape = []
    for k in devices:
        if k == 0:
            out_shape.append(jax.ShapeDtypeStruct((256, 256), f32))
            out_shape.append(jax.ShapeDtypeStruct((256, 256), bf16))
        else:
            out_shape.append(jax.ShapeDtypeStruct((256, 512), bf16))
    taken = [half for k in devices for half in halves[2 * k : 2 * k + 2]]
    return pl.pallas_call(
        functools.partial(last_kernel, devices),
        in_specs=scalars() + in_vmem(4 + len(taken)),
        out_specs=in_vmem(len(out_shape)),
        out_shape=out_shape,
        compiler_params=params(),
        cost_estimate=cost(2 * 256 * len(devices) * 128 * width, 1024 * width),
        name="value_parts",
    )(place, own, side, *taken, *gaps)


def join_kernel(place_ref, flag_ref, *refs):
    mine, over, out_ref, held = refs[:4], refs[4:8], refs[8], refs[9]
    c, p, q = place_ref[0], place_ref[1], place_ref[2]
    for d in range(4):
        held[c, (p + d) % 4] = mine[d][:, :256].astype(f32)
        held[1 - c, (q + d) % 4] = over[d][:, -256:].astype(f32)
    flag = flag_ref[...].astype(f32)
    for x in range(4):
        for j in range(2):
            near = held[0, x, :, j * 128 : (j + 1) * 128]
            far = jnp.concatenate(
                [
                    held[1, 2 * j, :, x * 64 : (x + 1) * 64],
                    held[1, 2 * j + 1, :, x * 64 : (x + 1) * 64],
                ],
                axis=1,
            )
            out_ref[:, x * 256 + j * 128 : x * 256 + (j + 1) * 128] = (near + far) * flag


def joined(place, flag, mine, over):
    vmem = pl.BlockSpec(memory_space=pltpu.VMEM)
    return pl.pallas_call(
        join_kernel,
        in_specs=[pl.BlockSpec(memory_space=pltpu.SMEM)] + [vmem] * 9,
        out_specs=vmem,
        out_shape=jax.ShapeDtypeStruct((256, 1024), f32),
        scratch_shapes=[pltpu.VMEM((2, 4, 256, 256), f32)],
        compiler_params=params(),
        name="joined",
    )(place, flag.reshape(256, 1), *mine, *over)


def body(
    fresh, replay_buffer, replay_index, from_replay, cotangent, master, moment1, moment2, teacher
):
    c, x, y = (lax.axis_index(a) for a in ("c", "x", "y"))
    p = jnp.where(c == 0, x, y)
    q = jnp.where(c == 0, y, x)
    place = jnp.stack([c, p, q]).astype(jnp.int32)
    total_rows = fresh.shape[0] * lax.axis_size(ROWS)

    up, down = first_ring(1), first_ring(-1)
    slot = jnp.where(from_replay == 1, replay_index, -1).reshape(1, -1)
    a, b, b_cot, a_cot, cot_own = shared(
        place, slot, replay_buffer, fresh, cotangent
    )
    left_a = send(a, up)
    right_b = send(b, down)
    left_b = send(b_cot, up)
    right_a = send(a_cot, down)
    far_a = send(left_a, up)
    far_b = send(right_b, down)
    halves = (a, b, right_a, right_b, left_a, left_b, far_a, far_b)
    near = near_grad(cot_own, halves[:6])
    far = (near, far_a, far_b)
    a2, b2 = grad_parts((256, 320), *far)
    am, bm, b1, a1, own = grad_parts((384, 448, 192, 128, 0), *far)

    up2, down2 = second_ring(1), second_ring(-1)
    pass_a = send(a2, up2)
    pass_b = send(b2, down2)
    got_b = send(b1, up2)
    got_a = send(am, down2)
    sum_a = send((a1.astype(f32) + pass_a.astype(f32)).astype(bf16), up2)
    sum_b = send((bm.astype(f32) + pass_b.astype(f32)).astype(bf16), down2)
    ring_sum = jnp.concatenate(
        [
            own[:64] + sum_a.astype(f32) + got_a.astype(f32),
            own[64:] + sum_b.astype(f32) + got_b.astype(f32),
        ],
        axis=0,
    ).astype(bf16)

    width = own.shape[1]
    slices = lax.all_to_all(ring_sum.reshape(8, 16, width), ("zl", "zh"), 0, 0, tiled=True)
    grad = jnp.sum(slices.astype(f32), axis=0)
    grad = grad * (1.0 / math.sqrt(total_rows))
    new_moment1 = beta_one * moment1 + (1.0 - beta_one) * grad
    new_moment2 = beta_two * moment2 + (1.0 - beta_two) * grad * grad
    new_master = master - learn_rate * (new_moment1 / corr_one) / (
        jnp.sqrt(new_moment2 / corr_two) + adam_eps
    )
    new_teacher = ema_decay * teacher + (1.0 - ema_decay) * new_master
    gap_low = (new_master - new_teacher).astype(bf16)

    copies = jnp.broadcast_to(gap_low[None], (8, 16, width))
    column = lax.all_to_all(copies, ("zl", "zh"), 0, 0, tiled=True)
    ga = column[:4].reshape(64, width)
    gb = column[4:].reshape(64, width)
    left_ga = send(ga, up2)
    right_gb = send(gb, down2)
    left_gb = send(gb, up2)
    right_ga = send(ga, down2)
    far_ga = send(left_ga, up2)
    far_gb = send(right_gb, down2)
    first = values(place, halves, (ga, gb))
    side = values(place, halves, (right_ga, right_gb, left_ga, left_gb))
    known = (place, first, side, halves, (far_ga, far_gb))

    (out_far,) = value_parts((3,), *known)
    from_far = send(out_far, first_ring(2))
    out_right, out_left, mine, over = value_parts((1, 2, 0), *known)
    from_left = send(out_right, up)
    from_right = send(out_left, down)
    got = (from_right, from_far, from_left)
    crossed = [send(part, other_core) for part in (over,) + got]
    teacher_out = joined(place, from_replay, (mine,) + got, crossed)
    return (new_master, new_moment1, new_moment2, new_teacher, teacher_out)


def solution(mesh):
    fine = Mesh(mesh.devices.reshape(SIZES), AXES)
    split = P(ROWS, "c")
    return jax.shard_map(
        body,
        mesh=fine,
        in_specs=(split, split, P(ROWS), P(ROWS), P(ROWS, None), split, split, split, split),
        out_specs=(split, split, split, split, split),
        check_vma=False,
    )
```

```python
import functools
import itertools
import math

import jax
import jax.numpy as jnp
from jax import lax
from jax.experimental import pallas as pl
from jax.experimental.pallas import tpu as pltpu
from jax.sharding import Mesh, PartitionSpec as P

beta_one = 0.9
beta_two = 0.999
learn_rate = 0.001
adam_eps = 1e-08
ema_decay = 0.99
corr_one = 1.0 - math.exp(100.0 * math.log(0.9))
corr_two = 1.0 - math.exp(100.0 * math.log(0.999))

bf16, f32 = jnp.bfloat16, jnp.float32
AXES = ("zl", "x", "y", "zh", "c")
SIZES = (2, 4, 4, 4, 2)
ROWS = tuple(AXES[:4])
VMEM_LIMIT = 16 * 1024 * 1024
SHARE_LIMIT = 50 * 1024 * 1024


def flat(zl, x, y, zh, c):
    return (((zl * 4 + x) * 4 + y) * 4 + zh) * 2 + c


def pairs(move):
    return [
        (flat(*place), flat(*move(*place)))
        for place in itertools.product(*map(range, SIZES))
    ]


def first_ring(s):
    return pairs(
        lambda zl, x, y, zh, c: (zl, (x + s) % 4, y, zh, c)
        if c == 0
        else (zl, x, (y + s) % 4, zh, c)
    )


def second_ring(s):
    return pairs(
        lambda zl, x, y, zh, c: (zl, x, (y + s) % 4, zh, c)
        if c == 0
        else (zl, (x + s) % 4, y, zh, c)
    )


other_core = pairs(lambda zl, x, y, zh, c: (zl, x, y, zh, 1 - c))


def send(array, perm):
    return lax.ppermute(array, AXES, perm)


def dot(lhs, rhs, left, right):
    return lax.dot_general(
        lhs, rhs, (((left,), (right,)), ((), ())), preferred_element_type=f32
    )


def params():
    return pltpu.CompilerParams(vmem_limit_bytes=VMEM_LIMIT)


def cost(flops, size):
    return pl.CostEstimate(flops=flops, bytes_accessed=size, transcendentals=0)


def in_vmem(count):
    return [pl.BlockSpec(memory_space=pltpu.VMEM)] * count


def scalars():
    return [pl.BlockSpec(memory_space=pltpu.SMEM)]


COLS = 256
WIDTH = 2304
TALL = WIDTH // COLS * 128


def share_kernel(*refs):
    place_ref, slot_ref, buffer_hbm, fresh_hbm, cot_hbm = refs[:5]
    a_ref, b_ref, up_ref, down_ref, own_ref = refs[5:10]
    buffer_ref, fresh_ref, cot_ref, turned, sems = refs[10:]
    slots, rows = buffer_ref.shape[0], fresh_ref.shape[0]
    width, half = fresh_ref.shape[1], fresh_ref.shape[0] // 2
    third = width // 3
    cot_copy = pltpu.make_async_copy(cot_hbm, cot_ref, sems.at[0])
    large = []
    for j in range(3):
        cut = (slice(None), pl.ds(j * third, third))
        large.append(
            (
                pltpu.make_async_copy(fresh_hbm.at[cut], fresh_ref.at[cut], sems.at[1 + j]),
                pltpu.make_async_copy(buffer_hbm.at[cut], buffer_ref.at[cut], sems.at[4 + j]),
            )
        )
    for copy in [cot_copy] + [copy for pair in large for copy in pair]:
        copy.start()

    wanted = slot_ref[...]
    slot = lax.broadcasted_iota(jnp.int32, (slots, rows), 0)
    pick = jnp.where(slot == wanted, 1.0, 0.0).astype(bf16).T
    same = lax.broadcasted_iota(jnp.int32, (rows, rows), 0) == lax.broadcasted_iota(
        jnp.int32, (rows, rows), 1
    )
    keep = jnp.where(same & (wanted < 0), 1.0, 0.0).astype(bf16).T

    cot_copy.wait()
    turned[...] = cot_ref[...].T
    c, p, q = place_ref[0], place_ref[1], place_ref[2]
    blocks = width // COLS
    for k in range(4):
        pk = (p + k) % 4
        for d in range(4):
            qd = (q + d) % 4
            x = jnp.where(c == 0, pk, qd)
            y = jnp.where(c == 0, qd, pk)
            if k == 2:
                target, base = (a_ref, b_ref)[d // 2], TALL + d % 2 * 128
            elif k == 0:
                target, base = own_ref, d * 128
            else:
                target, base = up_ref if k == 1 else down_ref, TALL + d * 128
            for zl in range(2):
                start = pl.multiple_of(zl * 1024 + x * 256 + y * 64, 64)
                target[pl.ds(base + zl * 64, 64), :] = turned[pl.ds(start, 64), :]

    for j in range(blocks):
        if j % (blocks // 3) == 0:
            for copy in large[j // (blocks // 3)]:
                copy.wait()
        cut = (slice(None), pl.ds(j * COLS, COLS))
        got = dot(pick, buffer_ref[cut], 1, 0) + dot(keep, fresh_ref[cut], 1, 0)
        got = got.astype(bf16)
        at = pl.ds(j * half, half)
        a_ref[at, :] = got[:half]
        down_ref[at, :] = got[:half]
        b_ref[at, :] = got[half:]
        up_ref[at, :] = got[half:]


def shared(place, slot, buffer, fresh, cot):
    rows, width = fresh.shape
    shapes = [(TALL + 256, COLS)] * 2 + [(TALL + 512, COLS)] * 2 + [(512, rows)]
    hbm = pl.BlockSpec(memory_space=pl.ANY)
    return pl.pallas_call(
        share_kernel,
        in_specs=scalars() + in_vmem(1) + [hbm] * 3,
        out_specs=in_vmem(5),
        out_shape=[jax.ShapeDtypeStruct(shape, bf16) for shape in shapes],
        scratch_shapes=[
            pltpu.VMEM(buffer.shape, bf16),
            pltpu.VMEM(fresh.shape, bf16),
            pltpu.VMEM(cot.shape, bf16),
            pltpu.VMEM((cot.shape[1], rows), bf16),
            pltpu.SemaphoreType.DMA((7,)),
        ],
        compiler_params=pltpu.CompilerParams(vmem_limit_bytes=SHARE_LIMIT),
        cost_estimate=cost(2 * 768 * rows * width, 8 * rows * width),
        name="shared",
    )(place, slot, buffer, fresh, cot)


def column_block(half, j):
    return half[pl.ds(pl.multiple_of(j * 128, 128), 128), :]


def all_columns(half):
    return jnp.concatenate([half[128 * j : 128 * (j + 1), :] for j in range(9)], axis=1)


def near_kernel(own_ref, *refs):
    halves, out_ref = refs[:6], refs[6]
    cots = (own_ref, halves[2].at[pl.ds(TALL, 512)], halves[5].at[pl.ds(TALL, 512)])

    @pl.loop(0, out_ref.shape[1] // COLS)
    def _(j):
        total = None
        for k in range(3):
            rows = jnp.concatenate(
                [column_block(halves[2 * k], j), column_block(halves[2 * k + 1], j)], axis=0
            )
            part = dot(cots[k][...], rows, 1, 0)
            total = part if total is None else total + part
        out_ref[:, pl.ds(pl.multiple_of(j * COLS, COLS), COLS)] = total


def near_grad(cot, halves):
    width = WIDTH
    return pl.pallas_call(
        near_kernel,
        in_specs=in_vmem(7),
        out_specs=in_vmem(1)[0],
        out_shape=jax.ShapeDtypeStruct((512, width), f32),
        compiler_params=params(),
        cost_estimate=cost(2 * 768 * 512 * width, 8 * 512 * width),
        name="near_grad",
    )(cot, *halves)


def far_kernel(starts, near_ref, a_ref, b_ref, *outs):
    @pl.loop(0, near_ref.shape[1] // COLS)
    def _(j):
        cut = (slice(None), pl.ds(pl.multiple_of(j * COLS, COLS), COLS))
        rows = jnp.concatenate([column_block(a_ref, j), column_block(b_ref, j)], axis=0)
        sums = {}
        for start, out in zip(starts, outs):
            chunk, low = start // 128, start % 128
            if chunk not in sums:
                at = slice(128 * chunk, 128 * chunk + 128)
                cot = (a_ref, b_ref)[chunk // 2][pl.ds(TALL + chunk % 2 * 128, 128), :]
                sums[chunk] = near_ref[at, cut[1]] + dot(cot, rows, 1, 0)
            out[cut] = sums[chunk][low : low + out.shape[0]].astype(out.dtype)


def grad_parts(starts, near, a, b):
    width = near.shape[1]
    out_shape = [
        jax.ShapeDtypeStruct((64, width), bf16)
        if start
        else jax.ShapeDtypeStruct((128, width), f32)
        for start in starts
    ]
    return pl.pallas_call(
        functools.partial(far_kernel, starts),
        in_specs=in_vmem(3),
        out_specs=in_vmem(len(starts)),
        out_shape=out_shape,
        compiler_params=params(),
        cost_estimate=cost(2 * 256 * 64 * len(starts) * width, 4 * 512 * width),
        name="grad_parts",
    )(near, a, b)


def own_first(c, a, b):
    return [jnp.where(c == 0, a, b), jnp.where(c == 0, b, a)]


def values_kernel(groups, place_ref, *refs):
    halves, gaps, out_ref = refs[:8], refs[8 : 8 + 2 * groups], refs[8 + 2 * groups]
    c = place_ref[0]
    gap = []
    for n in range(groups):
        gap += own_first(c, gaps[2 * n][...], gaps[2 * n + 1][...])
    gap = jnp.concatenate(gap, axis=0)
    for k in range(4):
        rows = jnp.concatenate(
            [all_columns(halves[2 * k]), all_columns(halves[2 * k + 1])], axis=0
        )
        out_ref[pl.ds(256 * k, 256), :] = dot(rows, gap, 1, 1)


def values(place, halves, gaps):
    groups, width = len(gaps) // 2, gaps[0].shape[1]
    return pl.pallas_call(
        functools.partial(values_kernel, groups),
        in_specs=scalars() + in_vmem(len(halves) + len(gaps)),
        out_specs=in_vmem(1)[0],
        out_shape=jax.ShapeDtypeStruct((1024, 128 * groups), f32),
        compiler_params=params(),
        cost_estimate=cost(2 * 1024 * 128 * groups * width, 4 * 1024 * width),
        name="values",
    )(place, *halves, *gaps)


def packed(q, tiles):
    pairs_of = lambda left, right, lo: jnp.concatenate(
        [left[:, lo : lo + 64], right[:, lo : lo + 64]], axis=1
    )
    both = []
    for lo in (0, 64):
        line = jnp.concatenate(
            [pairs_of(tiles[0], tiles[1], lo), pairs_of(tiles[2], tiles[3], lo)], axis=1
        )
        both.append(pltpu.roll(line, q * 64, 1))
    return both


def last_kernel(devices, place_ref, own_ref, side_ref, *refs):
    count = len(devices)
    halves, gaps, outs = refs[: 2 * count], refs[2 * count : 2 * count + 2], refs[2 * count + 2 :]
    c, q = place_ref[0], place_ref[2]
    gap = jnp.concatenate(own_first(c, gaps[0][...], gaps[1][...]), axis=0)
    for n, k in enumerate(devices):
        rows = jnp.concatenate(
            [all_columns(halves[2 * n]), all_columns(halves[2 * n + 1])], axis=0
        )
        part = dot(rows, gap, 1, 1)
        cut = pl.ds(256 * k, 256)
        side = side_ref[cut, :]
        mine, over = packed(q, (own_ref[cut, :], side[:, :128], part, side[:, 128:]))
        if k == 0:
            outs[n][...] = mine
            outs[n + 1][...] = over.astype(bf16)
        else:
            outs[n][:, :256] = mine.astype(bf16)
            outs[n][:, 256:] = over.astype(bf16)


def value_parts(devices, place, own, side, halves, gaps):
    width = gaps[0].shape[1]
    out_shape = []
    for k in devices:
        if k == 0:
            out_shape.append(jax.ShapeDtypeStruct((256, 256), f32))
            out_shape.append(jax.ShapeDtypeStruct((256, 256), bf16))
        else:
            out_shape.append(jax.ShapeDtypeStruct((256, 512), bf16))
    taken = [half for k in devices for half in halves[2 * k : 2 * k + 2]]
    return pl.pallas_call(
        functools.partial(last_kernel, devices),
        in_specs=scalars() + in_vmem(4 + len(taken)),
        out_specs=in_vmem(len(out_shape)),
        out_shape=out_shape,
        compiler_params=params(),
        cost_estimate=cost(2 * 256 * len(devices) * 128 * width, 1024 * width),
        name="value_parts",
    )(place, own, side, *taken, *gaps)


def join_kernel(place_ref, flag_ref, *refs):
    mine, over, out_ref, held = refs[:4], refs[4:8], refs[8], refs[9]
    c, p, q = place_ref[0], place_ref[1], place_ref[2]
    for d in range(4):
        held[c, (p + d) % 4] = mine[d][:, :256].astype(f32)
        held[1 - c, (q + d) % 4] = over[d][:, -256:].astype(f32)
    flag = flag_ref[...].astype(f32)
    for x in range(4):
        for j in range(2):
            near = held[0, x, :, j * 128 : (j + 1) * 128]
            far = jnp.concatenate(
                [
                    held[1, 2 * j, :, x * 64 : (x + 1) * 64],
                    held[1, 2 * j + 1, :, x * 64 : (x + 1) * 64],
                ],
                axis=1,
            )
            out_ref[:, x * 256 + j * 128 : x * 256 + (j + 1) * 128] = (near + far) * flag


def joined(place, flag, mine, over):
    vmem = pl.BlockSpec(memory_space=pltpu.VMEM)
    return pl.pallas_call(
        join_kernel,
        in_specs=[pl.BlockSpec(memory_space=pltpu.SMEM)] + [vmem] * 9,
        out_specs=vmem,
        out_shape=jax.ShapeDtypeStruct((256, 1024), f32),
        scratch_shapes=[pltpu.VMEM((2, 4, 256, 256), f32)],
        compiler_params=params(),
        name="joined",
    )(place, flag.reshape(256, 1), *mine, *over)


def body(
    fresh, replay_buffer, replay_index, from_replay, cotangent, master, moment1, moment2, teacher
):
    c, x, y = (lax.axis_index(a) for a in ("c", "x", "y"))
    p = jnp.where(c == 0, x, y)
    q = jnp.where(c == 0, y, x)
    place = jnp.stack([c, p, q]).astype(jnp.int32)
    total_rows = fresh.shape[0] * lax.axis_size(ROWS)

    up, down = first_ring(1), first_ring(-1)
    slot = jnp.where(from_replay == 1, replay_index, -1).reshape(1, -1)
    a, b, b_cot, a_cot, cot_own = shared(
        place, slot, replay_buffer, fresh, cotangent
    )
    left_a = send(a, up)
    right_b = send(b, down)
    left_b = send(b_cot, up)
    right_a = send(a_cot, down)
    far_a = send(left_a, up)
    far_b = send(right_b, down)
    halves = (a, b, right_a, right_b, left_a, left_b, far_a, far_b)
    near = near_grad(cot_own, halves[:6])
    far = (near, far_a, far_b)
    a2, b2 = grad_parts((256, 320), *far)
    am, bm, b1, a1, own = grad_parts((384, 448, 192, 128, 0), *far)

    up2, down2 = second_ring(1), second_ring(-1)
    pass_a = send(a2, up2)
    pass_b = send(b2, down2)
    got_b = send(b1, up2)
    got_a = send(am, down2)
    sum_a = send((a1.astype(f32) + pass_a.astype(f32)).astype(bf16), up2)
    sum_b = send((bm.astype(f32) + pass_b.astype(f32)).astype(bf16), down2)
    ring_sum = jnp.concatenate(
        [
            own[:64] + sum_a.astype(f32) + got_a.astype(f32),
            own[64:] + sum_b.astype(f32) + got_b.astype(f32),
        ],
        axis=0,
    ).astype(bf16)

    width = own.shape[1]
    slices = lax.all_to_all(ring_sum.reshape(8, 16, width), ("zl", "zh"), 0, 0, tiled=True)
    grad = jnp.sum(slices.astype(f32), axis=0)
    grad = grad * (1.0 / math.sqrt(total_rows))
    new_moment1 = beta_one * moment1 + (1.0 - beta_one) * grad
    new_moment2 = beta_two * moment2 + (1.0 - beta_two) * grad * grad
    new_master = master - learn_rate * (new_moment1 / corr_one) / (
        jnp.sqrt(new_moment2 / corr_two) + adam_eps
    )
    new_teacher = ema_decay * teacher + (1.0 - ema_decay) * new_master
    gap_low = (new_master - new_teacher).astype(bf16)

    copies = jnp.broadcast_to(gap_low[None], (8, 16, width))
    column = lax.all_to_all(copies, ("zl", "zh"), 0, 0, tiled=True)
    ga = column[:4].reshape(64, width)
    gb = column[4:].reshape(64, width)
    left_ga = send(ga, up2)
    right_gb = send(gb, down2)
    left_gb = send(gb, up2)
    right_ga = send(ga, down2)
    far_ga = send(left_ga, up2)
    far_gb = send(right_gb, down2)
    first = values(place, halves, (ga, gb))
    side = values(place, halves, (right_ga, right_gb, left_ga, left_gb))
    known = (place, first, side, halves, (far_ga, far_gb))

    out_far, out_right, out_left, mine, over = value_parts((3, 1, 2, 0), *known)
    from_far = send(out_far, first_ring(2))
    from_left = send(out_right, up)
    from_right = send(out_left, down)
    got = (from_right, from_far, from_left)
    crossed = [send(part, other_core) for part in (over,) + got]
    teacher_out = joined(place, from_replay, (mine,) + got, crossed)
    return (new_master, new_moment1, new_moment2, new_teacher, teacher_out)


def solution(mesh):
    fine = Mesh(mesh.devices.reshape(SIZES), AXES)
    split = P(ROWS, "c")
    return jax.shard_map(
        body,
        mesh=fine,
        in_specs=(split, split, P(ROWS), P(ROWS), P(ROWS, None), split, split, split, split),
        out_specs=(split, split, split, split, split),
        check_vma=False,
    )
```

```python
import functools
import itertools
import math

import jax
import jax.numpy as jnp
from jax import lax
from jax.experimental import pallas as pl
from jax.experimental.pallas import tpu as pltpu
from jax.sharding import Mesh, PartitionSpec as P

beta_one = 0.9
beta_two = 0.999
learn_rate = 0.001
adam_eps = 1e-08
ema_decay = 0.99
corr_one = 1.0 - math.exp(100.0 * math.log(0.9))
corr_two = 1.0 - math.exp(100.0 * math.log(0.999))

bf16, f32 = jnp.bfloat16, jnp.float32
AXES = ("zl", "x", "y", "zh", "c")
SIZES = (2, 4, 4, 4, 2)
ROWS = tuple(AXES[:4])
VMEM_LIMIT = 16 * 1024 * 1024
SHARE_LIMIT = 50 * 1024 * 1024


def flat(zl, x, y, zh, c):
    return (((zl * 4 + x) * 4 + y) * 4 + zh) * 2 + c


def pairs(move):
    return [
        (flat(*place), flat(*move(*place)))
        for place in itertools.product(*map(range, SIZES))
    ]


def first_ring(s):
    return pairs(
        lambda zl, x, y, zh, c: (zl, (x + s) % 4, y, zh, c)
        if c == 0
        else (zl, x, (y + s) % 4, zh, c)
    )


def second_ring(s):
    return pairs(
        lambda zl, x, y, zh, c: (zl, x, (y + s) % 4, zh, c)
        if c == 0
        else (zl, (x + s) % 4, y, zh, c)
    )


other_core = pairs(lambda zl, x, y, zh, c: (zl, x, y, zh, 1 - c))


def send(array, perm):
    return lax.ppermute(array, AXES, perm)


def dot(lhs, rhs, left, right):
    return lax.dot_general(
        lhs, rhs, (((left,), (right,)), ((), ())), preferred_element_type=f32
    )


def params():
    return pltpu.CompilerParams(vmem_limit_bytes=VMEM_LIMIT)


def cost(flops, size):
    return pl.CostEstimate(flops=flops, bytes_accessed=size, transcendentals=0)


def in_vmem(count):
    return [pl.BlockSpec(memory_space=pltpu.VMEM)] * count


def scalars():
    return [pl.BlockSpec(memory_space=pltpu.SMEM)]


COLS = 256
WIDTH = 2304
TALL = WIDTH // COLS * 128


def share_kernel(*refs):
    place_ref, slot_ref, buffer_hbm, fresh_hbm, cot_hbm = refs[:5]
    a_ref, b_ref, up_ref, down_ref, own_ref = refs[5:10]
    buffer_ref, fresh_ref, cot_ref, turned, sems = refs[10:]
    slots, rows = buffer_ref.shape[0], fresh_ref.shape[0]
    width, half = fresh_ref.shape[1], fresh_ref.shape[0] // 2
    third = width // 3
    cot_copy = pltpu.make_async_copy(cot_hbm, cot_ref, sems.at[0])
    large = []
    for j in range(3):
        cut = (slice(None), pl.ds(j * third, third))
        large.append(
            (
                pltpu.make_async_copy(fresh_hbm.at[cut], fresh_ref.at[cut], sems.at[1 + j]),
                pltpu.make_async_copy(buffer_hbm.at[cut], buffer_ref.at[cut], sems.at[4 + j]),
            )
        )
    for copy in [cot_copy] + [copy for pair in large for copy in pair]:
        copy.start()

    wanted = slot_ref[...]
    slot = lax.broadcasted_iota(jnp.int32, (slots, rows), 0)
    pick = jnp.where(slot == wanted, 1.0, 0.0).astype(bf16).T
    same = lax.broadcasted_iota(jnp.int32, (rows, rows), 0) == lax.broadcasted_iota(
        jnp.int32, (rows, rows), 1
    )
    keep = jnp.where(same & (wanted < 0), 1.0, 0.0).astype(bf16).T

    cot_copy.wait()
    turned[...] = cot_ref[...].T
    c, p, q = place_ref[0], place_ref[1], place_ref[2]
    blocks = width // COLS
    for k in range(4):
        pk = (p + k) % 4
        for d in range(4):
            qd = (q + d) % 4
            x = jnp.where(c == 0, pk, qd)
            y = jnp.where(c == 0, qd, pk)
            if k == 2:
                target, base = (a_ref, b_ref)[d // 2], TALL + d % 2 * 128
            elif k == 0:
                target, base = own_ref, d * 128
            else:
                target, base = up_ref if k == 1 else down_ref, TALL + d * 128
            for zl in range(2):
                start = pl.multiple_of(zl * 1024 + x * 256 + y * 64, 64)
                target[pl.ds(base + zl * 64, 64), :] = turned[pl.ds(start, 64), :]

    for j in range(blocks):
        if j % (blocks // 3) == 0:
            for copy in large[j // (blocks // 3)]:
                copy.wait()
        cut = (slice(None), pl.ds(j * COLS, COLS))
        got = dot(pick, buffer_ref[cut], 1, 0) + dot(keep, fresh_ref[cut], 1, 0)
        got = got.astype(bf16)
        at = pl.ds(j * half, half)
        a_ref[at, :] = got[:half]
        down_ref[at, :] = got[:half]
        b_ref[at, :] = got[half:]
        up_ref[at, :] = got[half:]


def shared(place, slot, buffer, fresh, cot):
    rows, width = fresh.shape
    shapes = [(TALL + 256, COLS)] * 2 + [(TALL + 512, COLS)] * 2 + [(512, rows)]
    hbm = pl.BlockSpec(memory_space=pl.ANY)
    return pl.pallas_call(
        share_kernel,
        in_specs=scalars() + in_vmem(1) + [hbm] * 3,
        out_specs=in_vmem(5),
        out_shape=[jax.ShapeDtypeStruct(shape, bf16) for shape in shapes],
        scratch_shapes=[
            pltpu.VMEM(buffer.shape, bf16),
            pltpu.VMEM(fresh.shape, bf16),
            pltpu.VMEM(cot.shape, bf16),
            pltpu.VMEM((cot.shape[1], rows), bf16),
            pltpu.SemaphoreType.DMA((7,)),
        ],
        compiler_params=pltpu.CompilerParams(vmem_limit_bytes=SHARE_LIMIT),
        cost_estimate=cost(2 * 768 * rows * width, 8 * rows * width),
        name="shared",
    )(place, slot, buffer, fresh, cot)


def column_block(half, j):
    return half[pl.ds(pl.multiple_of(j * 128, 128), 128), :]


def all_columns(half):
    return jnp.concatenate([half[128 * j : 128 * (j + 1), :] for j in range(9)], axis=1)


def near_kernel(own_ref, *refs):
    halves, out_ref = refs[:6], refs[6]
    cots = (own_ref, halves[2].at[pl.ds(TALL, 512)], halves[5].at[pl.ds(TALL, 512)])

    @pl.loop(0, out_ref.shape[1] // COLS)
    def _(j):
        total = None
        for k in range(3):
            rows = jnp.concatenate(
                [column_block(halves[2 * k], j), column_block(halves[2 * k + 1], j)], axis=0
            )
            part = dot(cots[k][...], rows, 1, 0)
            total = part if total is None else total + part
        out_ref[:, pl.ds(pl.multiple_of(j * COLS, COLS), COLS)] = total


def near_grad(cot, halves):
    width = WIDTH
    return pl.pallas_call(
        near_kernel,
        in_specs=in_vmem(7),
        out_specs=in_vmem(1)[0],
        out_shape=jax.ShapeDtypeStruct((512, width), f32),
        compiler_params=params(),
        cost_estimate=cost(2 * 768 * 512 * width, 8 * 512 * width),
        name="near_grad",
    )(cot, *halves)


def far_kernel(starts, near_ref, a_ref, b_ref, *outs):
    @pl.loop(0, near_ref.shape[1] // COLS)
    def _(j):
        cut = (slice(None), pl.ds(pl.multiple_of(j * COLS, COLS), COLS))
        rows = jnp.concatenate([column_block(a_ref, j), column_block(b_ref, j)], axis=0)
        sums = {}
        for start, out in zip(starts, outs):
            chunk, low = start // 128, start % 128
            if chunk not in sums:
                at = slice(128 * chunk, 128 * chunk + 128)
                cot = (a_ref, b_ref)[chunk // 2][pl.ds(TALL + chunk % 2 * 128, 128), :]
                sums[chunk] = near_ref[at, cut[1]] + dot(cot, rows, 1, 0)
            out[cut] = sums[chunk][low : low + out.shape[0]].astype(out.dtype)


def grad_parts(starts, near, a, b):
    width = near.shape[1]
    out_shape = [
        jax.ShapeDtypeStruct((64, width), bf16)
        if start
        else jax.ShapeDtypeStruct((128, width), f32)
        for start in starts
    ]
    return pl.pallas_call(
        functools.partial(far_kernel, starts),
        in_specs=in_vmem(3),
        out_specs=in_vmem(len(starts)),
        out_shape=out_shape,
        compiler_params=params(),
        cost_estimate=cost(2 * 256 * 64 * len(starts) * width, 4 * 512 * width),
        name="grad_parts",
    )(near, a, b)


def own_first(c, a, b):
    return [jnp.where(c == 0, a, b), jnp.where(c == 0, b, a)]


def values_kernel(groups, place_ref, *refs):
    halves, gaps, out_ref = refs[:8], refs[8 : 8 + 2 * groups], refs[8 + 2 * groups]
    c = place_ref[0]
    gap = []
    for n in range(groups):
        gap += own_first(c, gaps[2 * n][...], gaps[2 * n + 1][...])
    gap = jnp.concatenate(gap, axis=0)
    for k in range(4):
        rows = jnp.concatenate(
            [all_columns(halves[2 * k]), all_columns(halves[2 * k + 1])], axis=0
        )
        out_ref[pl.ds(256 * k, 256), :] = dot(rows, gap, 1, 1)


def values(place, halves, gaps):
    groups, width = len(gaps) // 2, gaps[0].shape[1]
    return pl.pallas_call(
        functools.partial(values_kernel, groups),
        in_specs=scalars() + in_vmem(len(halves) + len(gaps)),
        out_specs=in_vmem(1)[0],
        out_shape=jax.ShapeDtypeStruct((1024, 128 * groups), f32),
        compiler_params=params(),
        cost_estimate=cost(2 * 1024 * 128 * groups * width, 4 * 1024 * width),
        name="values",
    )(place, *halves, *gaps)


def packed(q, tiles):
    pairs_of = lambda left, right, lo: jnp.concatenate(
        [left[:, lo : lo + 64], right[:, lo : lo + 64]], axis=1
    )
    both = []
    for lo in (0, 64):
        line = jnp.concatenate(
            [pairs_of(tiles[0], tiles[1], lo), pairs_of(tiles[2], tiles[3], lo)], axis=1
        )
        both.append(pltpu.roll(line, q * 64, 1))
    return both


def last_kernel(devices, place_ref, own_ref, side_ref, *refs):
    count = len(devices)
    halves, gaps, outs = refs[: 2 * count], refs[2 * count : 2 * count + 2], refs[2 * count + 2 :]
    c, q = place_ref[0], place_ref[2]
    gap = jnp.concatenate(own_first(c, gaps[0][...], gaps[1][...]), axis=0)
    for n, k in enumerate(devices):
        rows = jnp.concatenate(
            [all_columns(halves[2 * n]), all_columns(halves[2 * n + 1])], axis=0
        )
        part = dot(rows, gap, 1, 1)
        cut = pl.ds(256 * k, 256)
        side = side_ref[cut, :]
        mine, over = packed(q, (own_ref[cut, :], side[:, :128], part, side[:, 128:]))
        if k == 0:
            outs[n][...] = mine
            outs[n + 1][...] = over.astype(bf16)
        else:
            outs[n][:, :256] = mine.astype(bf16)
            outs[n][:, 256:] = over.astype(bf16)


def value_parts(devices, place, own, side, halves, gaps):
    width = gaps[0].shape[1]
    out_shape = []
    for k in devices:
        if k == 0:
            out_shape.append(jax.ShapeDtypeStruct((256, 256), f32))
            out_shape.append(jax.ShapeDtypeStruct((256, 256), bf16))
        else:
            out_shape.append(jax.ShapeDtypeStruct((256, 512), bf16))
    taken = [half for k in devices for half in halves[2 * k : 2 * k + 2]]
    return pl.pallas_call(
        functools.partial(last_kernel, devices),
        in_specs=scalars() + in_vmem(4 + len(taken)),
        out_specs=in_vmem(len(out_shape)),
        out_shape=out_shape,
        compiler_params=params(),
        cost_estimate=cost(2 * 256 * len(devices) * 128 * width, 1024 * width),
        name="value_parts",
    )(place, own, side, *taken, *gaps)


def join_kernel(place_ref, flag_ref, *refs):
    mine, over, out_hbm, held, out_ref, sems = refs[:4], refs[4:8], *refs[8:]
    c, p, q = place_ref[0], place_ref[1], place_ref[2]
    for d in range(4):
        held[c, (p + d) % 4] = mine[d][:, :256].astype(bf16)
        held[1 - c, (q + d) % 4] = over[d][:, -256:]
    flag = flag_ref[...].astype(f32)
    copies = []
    for x in range(4):
        for j in range(2):
            near = held[0, x, :, j * 128 : (j + 1) * 128]
            far = jnp.concatenate(
                [
                    held[1, 2 * j, :, x * 64 : (x + 1) * 64],
                    held[1, 2 * j + 1, :, x * 64 : (x + 1) * 64],
                ],
                axis=1,
            )
            both = near.astype(f32) + far.astype(f32)
            out_ref[:, x * 256 + j * 128 : x * 256 + (j + 1) * 128] = both * flag
        cut = (slice(None), pl.ds(x * 256, 256))
        copies.append(pltpu.make_async_copy(out_ref.at[cut], out_hbm.at[cut], sems.at[x]))
        copies[-1].start()
    for copy in copies:
        copy.wait()


def joined(place, flag, mine, over):
    return pl.pallas_call(
        join_kernel,
        in_specs=scalars() + in_vmem(9),
        out_specs=pl.BlockSpec(memory_space=pl.ANY),
        out_shape=jax.ShapeDtypeStruct((256, 1024), f32),
        scratch_shapes=[
            pltpu.VMEM((2, 4, 256, 256), bf16),
            pltpu.VMEM((256, 1024), f32),
            pltpu.SemaphoreType.DMA((4,)),
        ],
        compiler_params=params(),
        name="joined",
    )(place, flag.reshape(256, 1), *mine, *over)


def body(
    fresh, replay_buffer, replay_index, from_replay, cotangent, master, moment1, moment2, teacher
):
    c, x, y = (lax.axis_index(a) for a in ("c", "x", "y"))
    p = jnp.where(c == 0, x, y)
    q = jnp.where(c == 0, y, x)
    place = jnp.stack([c, p, q]).astype(jnp.int32)
    total_rows = fresh.shape[0] * lax.axis_size(ROWS)

    up, down = first_ring(1), first_ring(-1)
    slot = jnp.where(from_replay == 1, replay_index, -1).reshape(1, -1)
    a, b, b_cot, a_cot, cot_own = shared(
        place, slot, replay_buffer, fresh, cotangent
    )
    left_a = send(a, up)
    right_b = send(b, down)
    left_b = send(b_cot, up)
    right_a = send(a_cot, down)
    far_a = send(left_a, up)
    far_b = send(right_b, down)
    halves = (a, b, right_a, right_b, left_a, left_b, far_a, far_b)
    near = near_grad(cot_own, halves[:6])
    far = (near, far_a, far_b)
    a2, b2 = grad_parts((256, 320), *far)
    am, bm, b1, a1, own = grad_parts((384, 448, 192, 128, 0), *far)

    up2, down2 = second_ring(1), second_ring(-1)
    pass_a = send(a2, up2)
    pass_b = send(b2, down2)
    got_b = send(b1, up2)
    got_a = send(am, down2)
    sum_a = send((a1.astype(f32) + pass_a.astype(f32)).astype(bf16), up2)
    sum_b = send((bm.astype(f32) + pass_b.astype(f32)).astype(bf16), down2)
    ring_sum = jnp.concatenate(
        [
            own[:64] + sum_a.astype(f32) + got_a.astype(f32),
            own[64:] + sum_b.astype(f32) + got_b.astype(f32),
        ],
        axis=0,
    ).astype(bf16)

    width = own.shape[1]
    slices = lax.all_to_all(ring_sum.reshape(8, 16, width), ("zl", "zh"), 0, 0, tiled=True)
    grad = jnp.sum(slices.astype(f32), axis=0)
    grad = grad * (1.0 / math.sqrt(total_rows))
    new_moment1 = beta_one * moment1 + (1.0 - beta_one) * grad
    new_moment2 = beta_two * moment2 + (1.0 - beta_two) * grad * grad
    new_master = master - learn_rate * (new_moment1 / corr_one) / (
        jnp.sqrt(new_moment2 / corr_two) + adam_eps
    )
    new_teacher = ema_decay * teacher + (1.0 - ema_decay) * new_master
    gap_low = (new_master - new_teacher).astype(bf16)

    copies = jnp.broadcast_to(gap_low[None], (8, 16, width))
    column = lax.all_to_all(copies, ("zl", "zh"), 0, 0, tiled=True)
    ga = column[:4].reshape(64, width)
    gb = column[4:].reshape(64, width)
    left_ga = send(ga, up2)
    right_gb = send(gb, down2)
    left_gb = send(gb, up2)
    right_ga = send(ga, down2)
    far_ga = send(left_ga, up2)
    far_gb = send(right_gb, down2)
    first = values(place, halves, (ga, gb))
    side = values(place, halves, (right_ga, right_gb, left_ga, left_gb))
    known = (place, first, side, halves, (far_ga, far_gb))

    out_far, out_right, out_left, mine, over = value_parts((3, 1, 2, 0), *known)
    from_far = send(out_far, first_ring(2))
    from_left = send(out_right, up)
    from_right = send(out_left, down)
    got = (from_right, from_far, from_left)
    crossed = [send(part, other_core) for part in (over,) + got]
    teacher_out = joined(place, from_replay, (mine,) + got, crossed)
    return (new_master, new_moment1, new_moment2, new_teacher, teacher_out)


def solution(mesh):
    fine = Mesh(mesh.devices.reshape(SIZES), AXES)
    split = P(ROWS, "c")
    return jax.shard_map(
        body,
        mesh=fine,
        in_specs=(split, split, P(ROWS), P(ROWS), P(ROWS, None), split, split, split, split),
        out_specs=(split, split, split, split, split),
        check_vma=False,
    )
```

```python
import functools
import itertools
import math

import jax
import jax.numpy as jnp
from jax import lax
from jax.experimental import pallas as pl
from jax.experimental.pallas import tpu as pltpu
from jax.sharding import Mesh, PartitionSpec as P

beta_one = 0.9
beta_two = 0.999
learn_rate = 0.001
adam_eps = 1e-08
ema_decay = 0.99
corr_one = 1.0 - math.exp(100.0 * math.log(0.9))
corr_two = 1.0 - math.exp(100.0 * math.log(0.999))

bf16, f32 = jnp.bfloat16, jnp.float32
AXES = ("zl", "x", "y", "zh", "c")
SIZES = (2, 4, 4, 4, 2)
ROWS = tuple(AXES[:4])
VMEM_LIMIT = 16 * 1024 * 1024
SHARE_LIMIT = 50 * 1024 * 1024


def flat(zl, x, y, zh, c):
    return (((zl * 4 + x) * 4 + y) * 4 + zh) * 2 + c


def pairs(move):
    return [
        (flat(*place), flat(*move(*place)))
        for place in itertools.product(*map(range, SIZES))
    ]


def first_ring(s):
    return pairs(
        lambda zl, x, y, zh, c: (zl, (x + s) % 4, y, zh, c)
        if c == 0
        else (zl, x, (y + s) % 4, zh, c)
    )


def second_ring(s):
    return pairs(
        lambda zl, x, y, zh, c: (zl, x, (y + s) % 4, zh, c)
        if c == 0
        else (zl, (x + s) % 4, y, zh, c)
    )


other_core = pairs(lambda zl, x, y, zh, c: (zl, x, y, zh, 1 - c))


def send(array, perm):
    return lax.ppermute(array, AXES, perm)


def dot(lhs, rhs, left, right):
    return lax.dot_general(
        lhs, rhs, (((left,), (right,)), ((), ())), preferred_element_type=f32
    )


def params():
    return pltpu.CompilerParams(vmem_limit_bytes=VMEM_LIMIT)


def cost(flops, size):
    return pl.CostEstimate(flops=flops, bytes_accessed=size, transcendentals=0)


def in_vmem(count):
    return [pl.BlockSpec(memory_space=pltpu.VMEM)] * count


def scalars():
    return [pl.BlockSpec(memory_space=pltpu.SMEM)]


COLS = 256
WIDTH = 2304
TALL = WIDTH // COLS * 128


def share_kernel(*refs):
    place_ref, slot_ref, buffer_hbm, fresh_hbm, cot_hbm = refs[:5]
    a_ref, b_ref, up_ref, down_ref, own_ref = refs[5:10]
    buffer_ref, fresh_ref, cot_ref, turned, sems = refs[10:]
    slots, rows = buffer_ref.shape[0], fresh_ref.shape[0]
    width, half = fresh_ref.shape[1], fresh_ref.shape[0] // 2
    third = width // 3
    cot_copy = pltpu.make_async_copy(cot_hbm, cot_ref, sems.at[0])
    large = []
    for j in range(3):
        cut = (slice(None), pl.ds(j * third, third))
        large.append(
            (
                pltpu.make_async_copy(fresh_hbm.at[cut], fresh_ref.at[cut], sems.at[1 + j]),
                pltpu.make_async_copy(buffer_hbm.at[cut], buffer_ref.at[cut], sems.at[4 + j]),
            )
        )
    for copy in [cot_copy] + [copy for pair in large for copy in pair]:
        copy.start()

    wanted = slot_ref[...]
    slot = lax.broadcasted_iota(jnp.int32, (slots, rows), 0)
    pick = jnp.where(slot == wanted, 1.0, 0.0).astype(bf16).T
    same = lax.broadcasted_iota(jnp.int32, (rows, rows), 0) == lax.broadcasted_iota(
        jnp.int32, (rows, rows), 1
    )
    keep = jnp.where(same & (wanted < 0), 1.0, 0.0).astype(bf16).T

    cot_copy.wait()
    turned[...] = cot_ref[...].T
    c, p, q = place_ref[0], place_ref[1], place_ref[2]
    blocks = width // COLS
    for k in range(4):
        pk = (p + k) % 4
        for d in range(4):
            qd = (q + d) % 4
            x = jnp.where(c == 0, pk, qd)
            y = jnp.where(c == 0, qd, pk)
            if k == 2:
                target, base = (a_ref, b_ref)[d // 2], TALL + d % 2 * 128
            elif k == 0:
                target, base = own_ref, d * 128
            else:
                target, base = up_ref if k == 1 else down_ref, TALL + d * 128
            for zl in range(2):
                start = pl.multiple_of(zl * 1024 + x * 256 + y * 64, 64)
                target[pl.ds(base + zl * 64, 64), :] = turned[pl.ds(start, 64), :]

    for j in range(blocks):
        if j % (blocks // 3) == 0:
            for copy in large[j // (blocks // 3)]:
                copy.wait()
        cut = (slice(None), pl.ds(j * COLS, COLS))
        got = dot(pick, buffer_ref[cut], 1, 0) + dot(keep, fresh_ref[cut], 1, 0)
        got = got.astype(bf16)
        at = pl.ds(j * half, half)
        a_ref[at, :] = got[:half]
        down_ref[at, :] = got[:half]
        b_ref[at, :] = got[half:]
        up_ref[at, :] = got[half:]


def shared(place, slot, buffer, fresh, cot):
    rows, width = fresh.shape
    shapes = [(TALL + 256, COLS)] * 2 + [(TALL + 512, COLS)] * 2 + [(512, rows)]
    hbm = pl.BlockSpec(memory_space=pl.ANY)
    return pl.pallas_call(
        share_kernel,
        in_specs=scalars() + in_vmem(1) + [hbm] * 3,
        out_specs=in_vmem(5),
        out_shape=[jax.ShapeDtypeStruct(shape, bf16) for shape in shapes],
        scratch_shapes=[
            pltpu.VMEM(buffer.shape, bf16),
            pltpu.VMEM(fresh.shape, bf16),
            pltpu.VMEM(cot.shape, bf16),
            pltpu.VMEM((cot.shape[1], rows), bf16),
            pltpu.SemaphoreType.DMA((7,)),
        ],
        compiler_params=pltpu.CompilerParams(vmem_limit_bytes=SHARE_LIMIT),
        cost_estimate=cost(2 * 768 * rows * width, 8 * rows * width),
        name="shared",
    )(place, slot, buffer, fresh, cot)


def column_block(half, j):
    return half[pl.ds(pl.multiple_of(j * 128, 128), 128), :]


def all_columns(half):
    return jnp.concatenate([half[128 * j : 128 * (j + 1), :] for j in range(9)], axis=1)


def near_kernel(own_ref, *refs):
    halves, out_ref = refs[:6], refs[6]
    cots = (own_ref, halves[2].at[pl.ds(TALL, 512)], halves[5].at[pl.ds(TALL, 512)])

    @pl.loop(0, out_ref.shape[1] // COLS)
    def _(j):
        total = None
        for k in range(3):
            rows = jnp.concatenate(
                [column_block(halves[2 * k], j), column_block(halves[2 * k + 1], j)], axis=0
            )
            part = dot(cots[k][...], rows, 1, 0)
            total = part if total is None else total + part
        out_ref[:, pl.ds(pl.multiple_of(j * COLS, COLS), COLS)] = total


def near_grad(cot, halves):
    width = WIDTH
    return pl.pallas_call(
        near_kernel,
        in_specs=in_vmem(7),
        out_specs=in_vmem(1)[0],
        out_shape=jax.ShapeDtypeStruct((512, width), f32),
        compiler_params=params(),
        cost_estimate=cost(2 * 768 * 512 * width, 8 * 512 * width),
        name="near_grad",
    )(cot, *halves)


def far_kernel(starts, near_ref, a_ref, b_ref, *outs):
    @pl.loop(0, near_ref.shape[1] // COLS)
    def _(j):
        cut = (slice(None), pl.ds(pl.multiple_of(j * COLS, COLS), COLS))
        rows = jnp.concatenate([column_block(a_ref, j), column_block(b_ref, j)], axis=0)
        sums = {}
        for start, out in zip(starts, outs):
            chunk, low = start // 128, start % 128
            if chunk not in sums:
                at = slice(128 * chunk, 128 * chunk + 128)
                cot = (a_ref, b_ref)[chunk // 2][pl.ds(TALL + chunk % 2 * 128, 128), :]
                sums[chunk] = near_ref[at, cut[1]] + dot(cot, rows, 1, 0)
            out[cut] = sums[chunk][low : low + out.shape[0]].astype(out.dtype)


def grad_parts(starts, near, a, b):
    width = near.shape[1]
    out_shape = [
        jax.ShapeDtypeStruct((64, width), bf16)
        if start
        else jax.ShapeDtypeStruct((128, width), f32)
        for start in starts
    ]
    return pl.pallas_call(
        functools.partial(far_kernel, starts),
        in_specs=in_vmem(3),
        out_specs=in_vmem(len(starts)),
        out_shape=out_shape,
        compiler_params=params(),
        cost_estimate=cost(2 * 256 * 64 * len(starts) * width, 4 * 512 * width),
        name="grad_parts",
    )(near, a, b)


def own_first(c, a, b):
    return [jnp.where(c == 0, a, b), jnp.where(c == 0, b, a)]


def values_kernel(groups, place_ref, *refs):
    halves, gaps, out_ref = refs[:8], refs[8 : 8 + 2 * groups], refs[8 + 2 * groups]
    c = place_ref[0]
    gap = []
    for n in range(groups):
        gap += own_first(c, gaps[2 * n][...], gaps[2 * n + 1][...])
    gap = jnp.concatenate(gap, axis=0)
    for k in range(4):
        rows = jnp.concatenate(
            [all_columns(halves[2 * k]), all_columns(halves[2 * k + 1])], axis=0
        )
        out_ref[pl.ds(256 * k, 256), :] = dot(rows, gap, 1, 1)


def values(place, halves, gaps):
    groups, width = len(gaps) // 2, gaps[0].shape[1]
    return pl.pallas_call(
        functools.partial(values_kernel, groups),
        in_specs=scalars() + in_vmem(len(halves) + len(gaps)),
        out_specs=in_vmem(1)[0],
        out_shape=jax.ShapeDtypeStruct((1024, 128 * groups), f32),
        compiler_params=params(),
        cost_estimate=cost(2 * 1024 * 128 * groups * width, 4 * 1024 * width),
        name="values",
    )(place, *halves, *gaps)


def packed(q, tiles):
    pairs_of = lambda left, right, lo: jnp.concatenate(
        [left[:, lo : lo + 64], right[:, lo : lo + 64]], axis=1
    )
    both = []
    for lo in (0, 64):
        line = jnp.concatenate(
            [pairs_of(tiles[0], tiles[1], lo), pairs_of(tiles[2], tiles[3], lo)], axis=1
        )
        both.append(pltpu.roll(line, q * 64, 1))
    return both


def last_kernel(devices, place_ref, own_ref, side_ref, *refs):
    count = len(devices)
    halves, gaps, outs = refs[: 2 * count], refs[2 * count : 2 * count + 2], refs[2 * count + 2 :]
    c, q = place_ref[0], place_ref[2]
    gap = jnp.concatenate(own_first(c, gaps[0][...], gaps[1][...]), axis=0)
    for n, k in enumerate(devices):
        rows = jnp.concatenate(
            [all_columns(halves[2 * n]), all_columns(halves[2 * n + 1])], axis=0
        )
        part = dot(rows, gap, 1, 1)
        cut = pl.ds(256 * k, 256)
        side = side_ref[cut, :]
        mine, over = packed(q, (own_ref[cut, :], side[:, :128], part, side[:, 128:]))
        if k == 0:
            outs[n][...] = mine
            outs[n + 1][...] = over.astype(bf16)
        else:
            outs[n][:, :256] = mine.astype(bf16)
            outs[n][:, 256:] = over.astype(bf16)


def value_parts(devices, place, own, side, halves, gaps):
    width = gaps[0].shape[1]
    out_shape = []
    for k in devices:
        if k == 0:
            out_shape.append(jax.ShapeDtypeStruct((256, 256), f32))
            out_shape.append(jax.ShapeDtypeStruct((256, 256), bf16))
        else:
            out_shape.append(jax.ShapeDtypeStruct((256, 512), bf16))
    taken = [half for k in devices for half in halves[2 * k : 2 * k + 2]]
    return pl.pallas_call(
        functools.partial(last_kernel, devices),
        in_specs=scalars() + in_vmem(4 + len(taken)),
        out_specs=in_vmem(len(out_shape)),
        out_shape=out_shape,
        compiler_params=params(),
        cost_estimate=cost(2 * 256 * len(devices) * 128 * width, 1024 * width),
        name="value_parts",
    )(place, own, side, *taken, *gaps)


def join_kernel(place_ref, flag_ref, *refs):
    mine, over, out_hbm, held, out_ref, sems = refs[:4], refs[4:8], *refs[8:]
    c, p, q = place_ref[0], place_ref[1], place_ref[2]
    for d in range(4):
        held[c, (p + d) % 4] = mine[d][:, :256].astype(f32)
        held[1 - c, (q + d) % 4] = over[d][:, -256:].astype(f32)
    flag = flag_ref[...].astype(f32)
    copies = []
    for x in range(4):
        for j in range(2):
            near = held[0, x, :, j * 128 : (j + 1) * 128]
            far = jnp.concatenate(
                [
                    held[1, 2 * j, :, x * 64 : (x + 1) * 64],
                    held[1, 2 * j + 1, :, x * 64 : (x + 1) * 64],
                ],
                axis=1,
            )
            both = near + far
            out_ref[:, x * 256 + j * 128 : x * 256 + (j + 1) * 128] = both * flag
        cut = (slice(None), pl.ds(x * 256, 256))
        copies.append(pltpu.make_async_copy(out_ref.at[cut], out_hbm.at[cut], sems.at[x]))
        copies[-1].start()
    for copy in copies:
        copy.wait()


def joined(place, flag, mine, over):
    return pl.pallas_call(
        join_kernel,
        in_specs=scalars() + in_vmem(9),
        out_specs=pl.BlockSpec(memory_space=pl.ANY),
        out_shape=jax.ShapeDtypeStruct((256, 1024), f32),
        scratch_shapes=[
            pltpu.VMEM((2, 4, 256, 256), f32),
            pltpu.VMEM((256, 1024), f32),
            pltpu.SemaphoreType.DMA((4,)),
        ],
        compiler_params=params(),
        name="joined",
    )(place, flag.reshape(256, 1), *mine, *over)


def body(
    fresh, replay_buffer, replay_index, from_replay, cotangent, master, moment1, moment2, teacher
):
    c, x, y = (lax.axis_index(a) for a in ("c", "x", "y"))
    p = jnp.where(c == 0, x, y)
    q = jnp.where(c == 0, y, x)
    place = jnp.stack([c, p, q]).astype(jnp.int32)
    total_rows = fresh.shape[0] * lax.axis_size(ROWS)

    up, down = first_ring(1), first_ring(-1)
    slot = jnp.where(from_replay == 1, replay_index, -1).reshape(1, -1)
    a, b, b_cot, a_cot, cot_own = shared(
        place, slot, replay_buffer, fresh, cotangent
    )
    left_a = send(a, up)
    right_b = send(b, down)
    left_b = send(b_cot, up)
    right_a = send(a_cot, down)
    far_a = send(left_a, up)
    far_b = send(right_b, down)
    halves = (a, b, right_a, right_b, left_a, left_b, far_a, far_b)
    near = near_grad(cot_own, halves[:6])
    far = (near, far_a, far_b)
    a2, b2 = grad_parts((256, 320), *far)
    am, bm, b1, a1, own = grad_parts((384, 448, 192, 128, 0), *far)

    up2, down2 = second_ring(1), second_ring(-1)
    pass_a = send(a2, up2)
    pass_b = send(b2, down2)
    got_b = send(b1, up2)
    got_a = send(am, down2)
    sum_a = send((a1.astype(f32) + pass_a.astype(f32)).astype(bf16), up2)
    sum_b = send((bm.astype(f32) + pass_b.astype(f32)).astype(bf16), down2)
    ring_sum = jnp.concatenate(
        [
            own[:64] + sum_a.astype(f32) + got_a.astype(f32),
            own[64:] + sum_b.astype(f32) + got_b.astype(f32),
        ],
        axis=0,
    ).astype(bf16)

    width = own.shape[1]
    slices = lax.all_to_all(ring_sum.reshape(8, 16, width), ("zl", "zh"), 0, 0, tiled=True)
    grad = jnp.sum(slices.astype(f32), axis=0)
    grad = grad * (1.0 / math.sqrt(total_rows))
    new_moment1 = beta_one * moment1 + (1.0 - beta_one) * grad
    new_moment2 = beta_two * moment2 + (1.0 - beta_two) * grad * grad
    new_master = master - learn_rate * (new_moment1 / corr_one) / (
        jnp.sqrt(new_moment2 / corr_two) + adam_eps
    )
    new_teacher = ema_decay * teacher + (1.0 - ema_decay) * new_master
    gap_low = (new_master - new_teacher).astype(bf16)

    copies = jnp.broadcast_to(gap_low[None], (8, 16, width))
    column = lax.all_to_all(copies, ("zl", "zh"), 0, 0, tiled=True)
    ga = column[:4].reshape(64, width)
    gb = column[4:].reshape(64, width)
    left_ga = send(ga, up2)
    right_gb = send(gb, down2)
    left_gb = send(gb, up2)
    right_ga = send(ga, down2)
    far_ga = send(left_ga, up2)
    far_gb = send(right_gb, down2)
    first = values(place, halves, (ga, gb))
    side = values(place, halves, (right_ga, right_gb, left_ga, left_gb))
    known = (place, first, side, halves, (far_ga, far_gb))

    out_far, out_right, out_left, mine, over = value_parts((3, 1, 2, 0), *known)
    from_far = send(out_far, first_ring(2))
    from_left = send(out_right, up)
    from_right = send(out_left, down)
    got = (from_right, from_far, from_left)
    crossed = [send(part, other_core) for part in (over,) + got]
    teacher_out = joined(place, from_replay, (mine,) + got, crossed)
    return (new_master, new_moment1, new_moment2, new_teacher, teacher_out)


def solution(mesh):
    fine = Mesh(mesh.devices.reshape(SIZES), AXES)
    split = P(ROWS, "c")
    return jax.shard_map(
        body,
        mesh=fine,
        in_specs=(split, split, P(ROWS), P(ROWS), P(ROWS, None), split, split, split, split),
        out_specs=(split, split, split, split, split),
        check_vma=False,
    )
```
